512 devices in a mesh: cell: 64 (over z, y), mem: 8 (over x, core).
Axes of the slice: x: 4, y: 4, z: 16, core: 2. Of those that a mesh axis runs over, the one named last changes fastest.
Arguments:
- hidden_states: bfloat16 [8, 32768, 1024], P('mem', 'cell'), may hold values from -16 to 16
- targets: bfloat16 [100, 32768], P(None, 'cell'), may hold values from -6 to 6
- cell_area: float32 [32768], P('cell'), may hold values from 0.25 to 4
- region_ids: int32 [32768], P('cell'), may hold values from 0 to 1023, never falling along the last dimension, each value on 1 to 64 neighbouring positions
- decoder_weight: bfloat16 [1024, 100], replicated, may hold values from -0.1875 to 0.1875
Outputs:
- grad_hidden: bfloat16 [8, 32768, 1024], P('mem', 'cell')
- grad_weight: float32 [1024, 100], replicated
The draws below stay inside these ranges and needn't reach their ends.
Inputs may be any that keep to these rules, and one draw needn't show every extreme that they name: `region_ids`: region ids never fall along the cells and rise by 0 or 1 from one cell to the next; every id occurs; each region holds 1 to 64 cells, some exactly 64.
All inputs are finite; a program needn't handle non-finite values.
Results may differ from the reference program's by a relative error of at most 0.0055.
The reference program's roundings to bfloat16 on the way (of `predicted` and `grad_pred`) count: a program that leaves them out, or rounds other values in their place, can miss the bound.
Values may be sent and summed in bfloat16 or wider, within the bound.
A program may use at most 64 MiB of HBM per device.

```python
import math
import jax
import jax.numpy as jnp
import numpy as np
from jax import lax

MEMBERS = 8
LAT = 1024
VARS = 100
CELLS = 32768
REGIONS = 1024


def raised(entries, own_key, source, target, shards_of, factor):
    def block_of(axis_at):
        return (jnp.arange(entries.shape[axis_at]) // (entries.shape[axis_at] // shards_of)).reshape((-1,) + (1,) * (entries.ndim - 1 - axis_at))

    first = jax.random.permutation(own_key, shards_of)[block_of(target)]
    far = (block_of(target) + shards_of // 2) % shards_of
    return jnp.where((block_of(source) == first) | (block_of(source) == far), factor * entries, entries)


def levels(rng, dims, shards, low, high):
    loudness = 1.0
    for axis_at, blocks in shards:
        heights = jax.random.uniform(jax.random.fold_in(jax.random.fold_in(rng, 6), axis_at), (blocks,), jnp.float32, low / len(shards), high / len(shards))
        loudness = loudness * jnp.repeat(jnp.exp(heights), dims[axis_at] // blocks).reshape((-1,) + (1,) * (len(dims) - 1 - axis_at))
    return loudness


def split_up(count, total, limit, slope):
    loads = [(1 << 20) // math.isqrt(rank ** slope) + 1 for rank in range(2, count + 1)]
    spare, given = total - limit - (count - 1), [1] * (count - 1)
    while spare > 0:
        free = [i for i in range(count - 1) if given[i] < limit]
        whole, left = sum([loads[i] for i in free]), spare
        for i in free:
            more = min(limit - given[i], max(1, left * loads[i] // whole), spare)
            given[i] = given[i] + more
            spare = spare - more
    return np.array([limit] + given)


def ragged_sizes(own_key, amount, total, limit, skew):
    if amount == 2:
        one = jax.random.randint(own_key, (), max(1, total - limit), min(limit, total - 1) + 1)
        return jnp.stack([one, total - one])
    tallies = jnp.asarray(split_up(amount, total, limit, skew), jnp.int32)
    pairs = (amount - 1) // 2
    giver, receiver = tallies[1:1 + 2 * pairs:2], tallies[2:2 + 2 * pairs:2]
    room = jnp.minimum(giver - 1, limit - receiver)
    shifted = jax.random.randint(jax.random.fold_in(own_key, 1), (pairs,), 0, 1 << 20) % (room + 1)
    tallies = tallies.at[1:1 + 2 * pairs:2].set(giver - shifted).at[2:2 + 2 * pairs:2].set(receiver + shifted)
    return tallies[jax.random.permutation(jax.random.fold_in(own_key, 2), amount)]


def normal_values(rng, extent, scale, most, split=(), kind=jnp.bfloat16):
    array = jax.random.normal(rng, extent, jnp.float32) * scale
    if len(split) > 0:
        array = levels(rng, extent, split, -0.22, 0.18) * array
    return jnp.clip(array, min=-most, max=most).astype(kind)


def noise_with(stream_key, shape, width, bound, split, heavy, held_as=jnp.bfloat16):
    entries = width * jax.random.normal(stream_key, shape, jnp.float32)
    if split:
        entries = entries * levels(stream_key, shape, split, -0.22, 0.18)
    return jnp.clip(raised(entries, jax.random.fold_in(stream_key, 3), *heavy), -bound, bound).astype(held_as)


def setup_inputs(seed: int = 0) -> dict:
    key_list = jax.random.split(jax.random.key(seed), 6)
    return {
        "hidden_states": noise_with(key_list[0], (MEMBERS, CELLS, LAT), 1.0, 16.0, ((0, 8), (1, 64)), (1, 2, 64, 4.0)),
        "targets": normal_values(key_list[1], (VARS, CELLS), 1.0, 6.0, ((1, 64),)),
        "cell_area": jnp.clip(jnp.exp(math.log(4.0) - 2.7725887 * jax.random.uniform(key_list[2], (CELLS,), jnp.float32) ** levels(key_list[2], (CELLS,), ((0, 64),), -0.2, 0.2)), 0.25, 4.0),
        "region_ids": jnp.searchsorted(jnp.cumsum(ragged_sizes(key_list[3], REGIONS, CELLS, 64, 0)), jnp.arange(CELLS), side="right").astype(jnp.int32),
        "decoder_weight": normal_values(key_list[4], (LAT, VARS), LAT ** -0.5, 0.1875),
    }


SMOOTH = 0.1

def fair_terms(ensemble, target):
    members = ensemble.shape[0]
    offset = ensemble - target[None]
    distance = jnp.sqrt(offset * offset + SMOOTH * SMOOTH)
    pair_slope = jnp.zeros(ensemble.shape, jnp.float32)
    for partner in range(members):
        spread_gap = ensemble - ensemble[partner][None]
        spread_size = jnp.sqrt(spread_gap * spread_gap + SMOOTH * SMOOTH)
        pair_slope = pair_slope + spread_gap / spread_size
    return offset / distance / members - pair_slope / (members * (members - 1))

def pooled_terms(pooled, members, var_count):
    region_area = pooled[:, -1]
    inverse = 1.0 / jnp.where(region_area > 0.0, region_area, 1.0)
    ensemble = pooled[:, :members * var_count].reshape(pooled.shape[0], members, var_count)
    ensemble = jnp.transpose(ensemble * inverse[:, None, None], (1, 0, 2))
    target = pooled[:, members * var_count:members * var_count + var_count] * inverse[:, None]
    return fair_terms(ensemble, target)

def reference(hidden_states, targets, cell_area, region_ids, decoder_weight):
    members = hidden_states.shape[0]
    var_count = targets.shape[0]
    cell_count = targets.shape[1]
    weight_wide = decoder_weight.astype(jnp.float32)
    highest = lax.Precision.HIGHEST

    def member_pred(member_states):
        product = jnp.dot(member_states.astype(jnp.float32), weight_wide, precision=highest)
        return product.T.astype(jnp.bfloat16)
    predicted = lax.map(member_pred, hidden_states)
    values = predicted.astype(jnp.float32)
    target = targets.astype(jnp.float32)
    slope_sum = fair_terms(values, target)
    columns = jnp.concatenate([(values * cell_area[None, None, :]).reshape(members * var_count, cell_count), target * cell_area[None, :], cell_area[None, :]], axis=0).T
    for factor, regions in ((1, cell_count // 32), (16, cell_count // 512), (256, cell_count // 8192)):
        parent = region_ids // factor
        pooled = jax.ops.segment_sum(columns, parent, num_segments=regions, indices_are_sorted=True)
        crps_slope = pooled_terms(pooled, members, var_count)
        slope_sum = slope_sum + jnp.transpose(jnp.take(crps_slope, parent, axis=1), (0, 2, 1))
    area_total = jnp.sum(cell_area)
    mean_area = area_total / cell_count
    grad_pred = ((cell_area / mean_area)[None, None, :] * slope_sum).astype(jnp.bfloat16)

    def member_grad(member_delta):
        product = jnp.dot(member_delta.astype(jnp.float32).T, weight_wide.T, precision=highest)
        return product.astype(jnp.bfloat16)
    grad_hidden = lax.map(member_grad, grad_pred)

    def member_weight(index):
        states = hidden_states[index].astype(jnp.float32)
        delta = grad_pred[index].astype(jnp.float32)
        return jnp.dot(states.T, delta.T, precision=highest)
    weight_total = lax.optimization_barrier(jnp.sum(lax.map(member_weight, jnp.arange(members, dtype=jnp.int32)), axis=0))
    grad_weight = weight_total / jnp.sqrt(jnp.mean(weight_total * weight_total) + 1e-06)
    return (grad_hidden, grad_weight)
```

```python
import functools

import jax
import jax.numpy as jnp
from jax import lax
from jax.experimental import pallas as pl
from jax.experimental.pallas import tpu as pltpu
from jax.sharding import PartitionSpec as P

MESH = pl.DeviceIdType.MESH
F32, BF16, I32 = jnp.float32, jnp.bfloat16, jnp.int32
SMOOTH = 0.1
MEMBERS = 8
VARS = 100
VB = 13
ALL_CELLS = 32768
VMEM_LIMIT = 32 * 1024 * 1024
NEAR = (-2, -1, 1, 2)
BLOCK = [(dx, dy, dz) for dx in (2, 1, 3, 0) for dy in (2, 1, 3, 0) for dz in (1, 0) if dx or dy or dz]
NEARBY = [(dy, dz) for dy in (2, 1, 3, 0) for dz in (1, 0) if dy or dz]
MEM_STEPS = (4, 3, 5, 2, 6, 1, 7)
FAR_FIRST = sorted(range(1, 16), key=lambda d: abs(d - 8))
P1, PY, PN, PZ, P3, RC, RB, SZ, GB, GC, H1, H2, CM, CO, COUNT = 0, 1, 2, 3, 4, 5, 7, 8, 9, 13, 14, 15, 16, 17, 18


def dot(a, b, left, right):
    return lax.dot_general(a, b, (((left,), (right,)), ((), ())), preferred_element_type=F32)


def iota(shape, axis):
    return lax.broadcasted_iota(I32, shape, axis)


def two_parts(a):
    high = a.astype(BF16).astype(F32)
    return high, (a - high).astype(BF16).astype(F32)


def slopes(members, target):
    ratio = lambda d: d * lax.rsqrt(d * d + SMOOTH * SMOOTH)
    pair = [None] * MEMBERS
    for m in range(MEMBERS):
        for n in range(m + 1, MEMBERS):
            term = ratio(members[m] - members[n])
            pair[m] = term if pair[m] is None else pair[m] + term
            pair[n] = -term if pair[n] is None else pair[n] - term
    return [
        ratio(members[m] - target) * (1.0 / MEMBERS) - pair[m] * (1.0 / (MEMBERS * (MEMBERS - 1)))
        for m in range(MEMBERS)
    ]


def packed_slopes(packed):
    width = packed.shape[1]
    members = [packed[m * 16 : m * 16 + 16] for m in range(MEMBERS)]
    row = iota((16, width), 0)
    target = jnp.zeros((16, width), F32)
    for v in range(VB):
        at = target_row(v)
        target = jnp.where(row == v, packed[at : at + 1], target)
    return jnp.concatenate(slopes(members, target), axis=0)


def target_row(v):
    return (v % 8) * 16 + 13 + v // 8


def pooled_slopes(packed):
    area = packed[15:16]
    return packed_slopes(packed * (1.0 / jnp.where(area > 0.0, area, 1.0)))


def kernel(
    hid_in, tgt_in, area_in, rid_in, w_in, gh, gw,
    hid, tgt, area, rid, w, wp, tx, xs, psend, precv, gsend, grecv, sum_high, sum_low, mid_high, mid_low, spread,
    fine, middle, total, msend, yrecv, nrecv, zsend, zrecv,
    csend, crecv, own, bsend, brecv, strip, full, hsend, h1, h2send, h2, coarse_send, coarse_mine, tile_send, tile, grad, load, send, recv, relay,
):
    me, ce = lax.axis_index("mem"), lax.axis_index("cell")
    x, core = lax.div(me, 2), lax.rem(me, 2)
    z, y = lax.div(ce, 4), lax.rem(ce, 4)
    mem_peer = lambda d: {"mem": lax.rem(me + d, 8)}
    core_peer = {"mem": me + 1 - 2 * core}
    pair = lax.rem(z, 2)
    block_peer = lambda dx, dy, dz: {
        "mem": lax.rem(x + dx, 4) * 2 + core, "cell": (z + dz * (1 - 2 * pair)) * 4 + lax.rem(y + dy, 4)
    }
    y_peer = lambda d: {"cell": z * 4 + lax.rem(y + d, 4)}
    z_peer = lambda d: {"cell": lax.rem(z + d, 16) * 4 + y}
    near_peer = lambda d: {"cell": lax.rem(ce + 64 + d, 64)}

    def copy(source, landing, s, r, peer):
        return pltpu.make_async_remote_copy(
            src_ref=source, dst_ref=landing, send_sem=send.at[s], recv_sem=recv.at[r],
            device_id=peer, device_id_type=MESH,
        )

    def arrived(array, group):
        copy(array, array, group, group, core_peer).wait_recv()

    def sent(array, group):
        copy(array, array, group, group, core_peer).wait_send()

    def started(copies):
        for c in copies:
            c.start()
        return copies

    loads = [
        pltpu.make_async_copy(source, landing, load.at[i])
        for i, (source, landing) in enumerate([
            (w_in, w), (hid_in.at[0, pl.ds(0, 256)], hid.at[pl.ds(0, 256)]),
            (hid_in.at[0, pl.ds(256, 256)], hid.at[pl.ds(256, 256)]), (tgt_in, tgt), (area_in, area), (rid_in, rid),
        ])
    ]
    started(loads)
    barrier = pltpu.get_barrier_semaphore()
    peers = [mem_peer(d) for d in range(1, 8)] + [y_peer(d) for d in range(1, 4)]
    peers += [z_peer(1), z_peer(15)] + [near_peer(d) for d in NEAR]
    peers += [block_peer(0, dy, 1) for dy in (1, 2, 3)]
    for peer in peers:
        pl.semaphore_signal(barrier, inc=1, device_id=peer, device_id_type=MESH)

    row, col = iota((128, VARS), 0), iota((128, VARS), 1)
    block, place = lax.shift_right_logical(row, 4), row & 15
    pick = jnp.where((col == block * VB + place) & (place < VB), 1.0, 0.0).astype(BF16)
    loads[0].wait()
    wp[...] = dot(pick, w[...], 1, 0).astype(BF16)
    for i in range(2):
        loads[1 + i].wait()
        cells = slice(256 * i, 256 * i + 256)
        pred = dot(wp[...], hid[cells], 1, 1).astype(BF16)
        psend[:, :, cells] = pred.reshape(MEMBERS, 16, 256)

    def tell(step):
        for side in (1, -1):
            peer = z_peer(16 + side * 2**step)
            pl.semaphore_signal(relay.at[step], inc=1, device_id=peer, device_id_type=MESH)

    def hear(step):
        pl.semaphore_wait(relay.at[step], 2)

    pl.semaphore_wait(barrier, len(peers))
    started([
        copy(psend.at[lax.rem(me + d, 8)], precv.at[me], P1, P1, mem_peer(d))
        for d in MEM_STEPS
    ])
    tell(0)
    precv[pl.ds(me, 1)] = psend[pl.ds(me, 1)]

    for c in loads[3:]:
        c.wait()
    spot = jnp.where(place == 13, block, jnp.where((place == 14) & (block < VB - 8), block + 8, -1000))
    pick = jnp.where((spot >= 0) & (col == VB * me + spot), 1.0, 0.0).astype(BF16)
    tx[...] = dot(pick, tgt[...], 1, 0) + jnp.where(iota((128, 512), 0) == 15, 1.0, 0.0)

    ids = rid[...]
    mids, coarses = lax.shift_right_logical(ids, 4), lax.shift_right_logical(ids, 8)
    row = iota((8, 512), 0)
    key = jnp.where(row < 2, ids, jnp.where(row < 4, mids, coarses))
    ends = jnp.where(row % 2 == 0, key[:, 0:1], key[:, 511:512])
    label = jnp.where(row < 4, ends, row - 4)
    edge_high, edge_low = two_parts(jnp.where(key == label, area[...], 0.0))
    edge = jnp.concatenate([edge_high, edge_low], axis=0).astype(BF16)
    label_lane = jnp.where((iota((8, 128), 1) == 31) & (iota((8, 128), 0) < 4), label[:, 0:128].astype(F32), 0.0)

    turned = lambda a: jnp.transpose(jnp.broadcast_to(a, (128, 512)))
    ids_col = turned(ids.astype(F32))
    high_col, low_col = two_parts(turned(area[...]))
    for j in range(4):
        lanes = slice(128 * j, 128 * j + 128)
        same = ids_col == ids[:, lanes].astype(F32)
        sum_high[:, lanes] = jnp.where(same, high_col, 0.0).astype(BF16)
        sum_low[:, lanes] = jnp.where(same, low_col, 0.0).astype(BF16)
    first_id, last_id = ids[:, 0:1], ids[:, 511:512]
    first_mid, last_mid = mids[:, 0:1], mids[:, 511:512]
    same = lax.shift_right_logical(ids_col.astype(I32), 4) == iota((512, 128), 1) + first_mid
    mid_high[...] = jnp.where(same, high_col, 0.0).astype(BF16)
    mid_low[...] = jnp.where(same, low_col, 0.0).astype(BF16)
    inner = (mids == iota((128, 512), 0) + first_mid) & (mids != first_mid) & (mids != last_mid)
    spread[...] = jnp.where(inner, 1.0, 0.0).astype(BF16)

    hear(0)
    tell(1)
    arrived(precv.at[pl.ds(0, 7)], P1)
    values = (precv[...].reshape(128, 512).astype(F32) + tx[...]).astype(BF16)
    xs[...] = values
    pooled = dot(edge, values, 1, 1)
    msend[...] = pooled[0:8] + pooled[8:16] + label_lane
    started([
        copy(msend, nrecv.at[k], PN, PN, near_peer(d)) for k, d in enumerate(NEAR)
    ])

    started([
        copy(msend, yrecv.at[d - 1], PY, PY, y_peer(d)) for d in range(1, 4)
    ])
    hear(1)
    tell(2)
    kept = (iota((128, 128), 0) & 15) < VB
    fine[...] = dot(values, sum_high[...], 1, 0) + dot(values, sum_low[...], 1, 0)
    table = pooled_slopes(dot(values, mid_high[...], 1, 0) + dot(values, mid_low[...], 1, 0))
    table_high, table_low = two_parts(table)
    middle[...] = dot(table_high.astype(BF16), spread[...], 1, 0) + dot(table_low.astype(BF16), spread[...], 1, 0)

    def inner_slopes(j, carry):
        lanes = pl.ds(pl.multiple_of(j * 128, 128), 128)
        here = rid[:, lanes]
        alone = (here != first_id) & (here != last_id)
        slope = packed_slopes(xs[:, lanes].astype(F32)) + middle[:, lanes]
        total[:, lanes] = slope + jnp.where(alone, pooled_slopes(fine[:, lanes]), 0.0)
        return carry

    lax.fori_loop(0, 4, inner_slopes, 0)

    arrived(nrecv, PN)
    after_2, after, before, before_2 = [nrecv[k] for k in range(4)]
    edges = msend[...]

    def joined(at, others):
        line = edges[at : at + 1]
        for other in others:
            line = line + jnp.where(other[:, 31:32] == edges[at : at + 1, 31:32], other, 0.0)
        return line

    around = [before[3:4], before_2[3:4], after[2:3], after_2[2:3]]
    lines = [joined(0, [before[1:2]]), joined(1, [after[0:1]]), joined(2, around), joined(3, around)]
    ends = pooled_slopes(jnp.transpose(jnp.concatenate(lines + [jnp.zeros((124, 128), F32)], axis=0)))
    columns = [jnp.broadcast_to(ends[:, k : k + 1], (128, 128)) for k in range(4)]

    def all_slopes(j, carry):
        lanes = pl.ds(pl.multiple_of(j * 128, 128), 128)
        here = rid[:, lanes]
        mid = lax.shift_right_logical(here, 4)
        slope = total[:, lanes]
        slope = slope + jnp.where(here == first_id, columns[0], jnp.where(here == last_id, columns[1], 0.0))
        slope = slope + jnp.where(mid == first_mid, columns[2], jnp.where(mid == last_mid, columns[3], 0.0))
        part = jnp.where(kept, area[:, lanes] * slope, 0.0)
        gsend[:, :, lanes] = part.astype(BF16).reshape(MEMBERS, 16, 128)
        return carry

    lax.fori_loop(0, 4, all_slopes, 0)
    started([
        copy(gsend.at[lax.rem(me + d, 8)], grecv.at[me], P3, P3, mem_peer(d))
        for d in MEM_STEPS
    ])
    grecv[pl.ds(me, 1)] = gsend[pl.ds(me, 1)]

    hear(2)
    arrived(yrecv, PY)
    zsend[...] = (msend[...] + yrecv[0] + yrecv[1] + yrecv[2])[4:8]
    started([
        copy(zsend, zrecv.at[d - 1], PZ, PZ, z_peer(d)) for d in FAR_FIRST
    ])
    moment = dot(edge, hid[...], 1, 0)
    moment = (moment[0:8] + moment[8:16])[4:8]
    for j in range(8):
        at = 128 * ((j % 2) * 4 + j // 2)
        hsend[j] = moment[:, at : at + 128]
    started([
        copy(hsend.at[lax.rem(me + d, 8)], h1.at[me], H1, H1, mem_peer(d)) for d in MEM_STEPS
    ])
    h1[pl.ds(me, 1)] = hsend[pl.ds(me, 1)]
    arrived(grecv.at[pl.ds(0, 7)], P3)
    delta = grecv[...].reshape(128, 512)

    def weight_part(half, k):
        lanes = pl.ds(pl.multiple_of(half * 512 + 256 * k, 256), 256)
        product = dot(delta, hid[:, lanes], 1, 0)
        return [product[:, 128 * i : 128 * i + 128].reshape(8, 16, 128) for i in range(2)]

    cc = []
    for k in range(2):
        for i, part in enumerate(weight_part(1 - core, k)):
            csend[2 * k + i] = part.astype(BF16)
        cc += started([
            copy(csend.at[pl.ds(2 * k, 2)], crecv.at[pl.ds(2 * k, 2)], RC + k, RC + k, core_peer)
        ])
    for k in range(2):
        for i, part in enumerate(weight_part(core, k)):
            own[2 * k + i] = part
    def block_copy(dx, dy, dz):
        slot = (dx * 4 + dy) * 2 + dz
        to = lax.rem(x + dx, 4), 2 * lax.rem(y + dy, 4) + pair + dz * (1 - 2 * pair)
        return copy(bsend.at[to], brecv.at[slot], RB, RB, block_peer(dx, dy, dz))

    for k in range(2):
        cc[k].wait_recv()
        for i in (2 * k, 2 * k + 1):
            both = own[i] + crecv[i].astype(F32)
            own[i] = both
            bsend[i] = both.astype(BF16)
        for i in (2 * k, 2 * k + 1):
            dx = lax.rem(i - x + 4, 4)
            for dy, dz in NEARBY:
                block_copy(dx, dy, dz).start()

            @pl.when(dx != 0)
            def _():
                block_copy(dx, 0, 0).start()

    arrived(h1.at[pl.ds(0, 7)], H1)
    moments = jnp.concatenate([h1[m] for m in range(8)], axis=0)
    h2send[...] = moments.astype(BF16)
    started([
        copy(h2send, h2.at[i], H2, H2, block_peer(0, dy, dz)) for i, (dy, dz) in enumerate(NEARBY)
    ])
    arrived(zrecv, PZ)
    coarse_sum = zsend[...]
    for d in range(15):
        coarse_sum = coarse_sum + zrecv[d]
    coarse = jnp.transpose(jnp.concatenate([coarse_sum, jnp.zeros((124, 128), F32)], axis=0))
    inverse_area = ALL_CELLS / jnp.sum(coarse[15:16, 0:4], axis=1, keepdims=True)
    coarse_slope = jnp.where(kept, pooled_slopes(coarse), 0.0).reshape(MEMBERS, 16, 128)
    tile_send[...] = jnp.concatenate(
        [coarse_slope[m, :, 0:4] for m in range(MEMBERS)] + [jnp.zeros((16, 96), F32)], axis=1
    )
    coarse_send[...] = coarse_slope
    row_block = 2 * y + pair
    to_owner = [copy(tile_send, tile, CO, CO, mem_peer(d)) for d in MEM_STEPS]

    @pl.when(me == row_block)
    def _():
        started(to_owner)
        tile[...] = tile_send[...]

    arrived(h2, H2)
    for i in range(7):
        moments = moments + h2[i].astype(F32)

    @pl.when(me != row_block)
    def _():
        to_owner[0].wait_recv()

    piece = own[x, 2 * y + pair]
    share = tile[...]
    for i in range(32):
        piece = piece + share[:, i : i + 1] * moments[i : i + 1, :]
    arrived(brecv.at[pl.ds(1, 31)], RB)
    for dx, dy, dz in BLOCK:
        piece = piece + brecv[(dx * 4 + dy) * 2 + dz].astype(F32)
    piece = piece * inverse_area

    layer = lax.div(z, 2)
    strip[layer] = piece.astype(BF16)
    started([
        copy(
            strip.at[layer], strip.at[layer], SZ, SZ,
            {"cell": (lax.rem(layer + d, 8) * 2 + pair) * 4 + y},
        )
        for d in (4, 3, 5, 2, 6, 1, 7)
    ])
    started([
        copy(coarse_send.at[lax.rem(me + d, 8)], coarse_mine.at[me], CM, CM, mem_peer(d))
        for d in MEM_STEPS
    ])
    coarse_mine[pl.ds(me, 1)] = coarse_send[pl.ds(me, 1)]
    sent(psend.at[pl.ds(0, 7)], P1)
    sent(nrecv, PN)
    sent(yrecv, PY)
    sent(gsend.at[pl.ds(0, 7)], P3)
    sent(zrecv, PZ)
    sent(h1.at[pl.ds(0, 7)], H1)
    sent(h2, H2)
    sent(brecv.at[pl.ds(1, 31)], RB)
    for c in cc:
        c.wait_send()

    @pl.when(me == row_block)
    def _():
        sent(coarse_send.at[pl.ds(0, 7)], CO)

    arrived(coarse_mine.at[pl.ds(0, 7)], CM)
    sent(coarse_send.at[pl.ds(0, 7)], CM)
    columns = [jnp.broadcast_to(coarse_mine[...].reshape(128, 128)[:, k : k + 1], (128, 128)) for k in range(4)]

    def gradient(j, carry):
        lanes = pl.ds(pl.multiple_of(j * 128, 128), 128)
        key = lax.shift_right_logical(rid[:, lanes], 8)
        slope = jnp.zeros((128, 128), F32)
        for k in range(4):
            slope = jnp.where(key == k, columns[k], slope)
        part = grecv[:, :, lanes].reshape(128, 128).astype(F32)
        grad[:, lanes] = ((part + area[:, lanes] * slope) * inverse_area).astype(BF16)
        return carry

    lax.fori_loop(0, 4, gradient, 0)
    gh[0] = dot(grad[...], wp[...], 0, 0).astype(BF16)
    arrived(strip.at[pl.ds(0, 7)], SZ)
    piece = strip[0].astype(F32)
    for k in range(1, 8):
        piece = piece + strip[k].astype(F32)
    chunk = core * 4 + x
    full[chunk, row_block] = piece.astype(BF16)

    spot = full.at[chunk, row_block]
    started([copy(spot, spot, GB, GB + at[0], block_peer(*at)) for i, at in enumerate(BLOCK)])
    sent(strip.at[pl.ds(0, 7)], SZ)
    for dx in (0, 1, 3, 2):
        arrived(full.at[0, pl.ds(0, 8 if dx else 7)], GB + dx)
        spot = full.at[core * 4 + lax.rem(x - dx + 4, 4)]
        started([copy(spot, spot, GC, GC, core_peer)])
    sent(brecv.at[pl.ds(1, 31)], GB)
    arrived(full.at[pl.ds(0, 4)], GC)

    square = jnp.zeros((16, 128), F32)
    for k in range(8):
        part = full[k].astype(F32)
        square = square + jnp.sum(part * part, axis=0)
    mean_square = jnp.sum(square, keepdims=True) * (1.0 / (VARS * 1024))
    scale = lax.rsqrt(mean_square + 1e-06)
    for k in range(8):
        for j in range(8):
            rows = min(VB, VARS - VB * j)
            gw[VB * j : VB * j + rows, 128 * k : 128 * k + 128] = (full[k, j].astype(F32) * scale)[0:rows]

    sent(full.at[pl.ds(0, 4)], GC)


def write_out(gh, gw, gh_out, gw_out, done):
    copies = [pltpu.make_async_copy(gh, gh_out, done.at[0]), pltpu.make_async_copy(gw, gw_out, done.at[1])]
    for c in copies:
        c.start()
    for c in copies:
        c.wait()


def local(hidden_states, targets, cell_area, region_ids, decoder_weight):
    anywhere = pl.BlockSpec(memory_space=pl.ANY)
    vmem = pl.BlockSpec(memory_space=pltpu.VMEM)
    scratch = [
        ((512, 1024), BF16), ((VARS, 512), BF16), ((1, 512), F32), ((1, 512), I32), ((VARS, 1024), BF16),
        ((128, 1024), BF16), ((128, 512), F32), ((128, 512), BF16),
        ((8, 16, 512), BF16), ((8, 16, 512), BF16), ((8, 16, 512), BF16), ((8, 16, 512), BF16),
        ((512, 512), BF16), ((512, 512), BF16), ((512, 128), BF16), ((512, 128), BF16), ((128, 512), BF16),
        ((128, 512), F32), ((128, 512), F32), ((128, 512), F32),
        ((8, 128), F32), ((3, 8, 128), F32), ((4, 8, 128), F32), ((4, 128), F32), ((15, 4, 128), F32),
        ((4, 8, 16, 128), BF16), ((4, 8, 16, 128), BF16), ((4, 8, 16, 128), F32), ((4, 8, 16, 128), BF16),
        ((32, 16, 128), BF16), ((8, 16, 128), BF16), ((8, 8, 16, 128), BF16),
        ((8, 4, 128), F32), ((8, 4, 128), F32), ((32, 128), BF16), ((7, 32, 128), BF16),
        ((8, 16, 128), F32), ((8, 16, 128), F32), ((16, 128), F32), ((16, 128), F32), ((128, 512), BF16),
    ]
    arguments = (
        hidden_states, targets, cell_area.reshape(1, -1), region_ids.reshape(1, -1), decoder_weight.T
    )
    results = (
        jax.ShapeDtypeStruct(hidden_states.shape, BF16),
        jax.ShapeDtypeStruct((VARS, 1024), F32),
    )
    grad_hidden, grad_weight = pl.pallas_call(
        kernel,
        out_shape=results,
        in_specs=[anywhere] * 5,
        out_specs=(vmem, vmem),
        scratch_shapes=[pltpu.VMEM(s, t) for s, t in scratch]
        + [pltpu.SemaphoreType.DMA((n,)) for n in (6, COUNT, COUNT)]
        + [pltpu.SemaphoreType.REGULAR((3,))],
        compiler_params=pltpu.CompilerParams(
            collective_id=0, has_side_effects=True, vmem_limit_bytes=VMEM_LIMIT
        ),
    )(*[pltpu.with_memory_space_constraint(a, pltpu.HBM) for a in arguments])
    grad_hidden, grad_weight = pl.pallas_call(
        write_out,
        out_shape=results,
        in_specs=[vmem] * 2,
        out_specs=(anywhere, anywhere),
        scratch_shapes=[pltpu.SemaphoreType.DMA((2,))],
    )(*[pltpu.with_memory_space_constraint(a, pltpu.VMEM) for a in (grad_hidden, grad_weight)])
    return grad_hidden, grad_weight.T


def solution(mesh):
    in_specs = (P("mem", "cell", None), P(None, "cell"), P("cell"), P("cell"), P())
    out_specs = (P("mem", "cell", None), P())
    return jax.shard_map(local, mesh=mesh, in_specs=in_specs, out_specs=out_specs, check_vma=False)
```

```python
import functools

import jax
import jax.numpy as jnp
from jax import lax
from jax.experimental import pallas as pl
from jax.experimental.pallas import tpu as pltpu
from jax.sharding import PartitionSpec as P

MESH = pl.DeviceIdType.MESH
F32, BF16, I32 = jnp.float32, jnp.bfloat16, jnp.int32
SMOOTH = 0.1
MEMBERS = 8
VARS = 100
VB = 13
ALL_CELLS = 32768
VMEM_LIMIT = 32 * 1024 * 1024
NEAR = (-2, -1, 1, 2)
BLOCK = [(dx, dy, dz) for dx in (2, 1, 3, 0) for dy in (2, 1, 3, 0) for dz in (1, 0) if dx or dy or dz]
NEARBY = [(dy, dz) for dy in (2, 1, 3, 0) for dz in (1, 0) if dy or dz]
MEM_STEPS = (4, 3, 5, 2, 6, 1, 7)
FAR_FIRST = sorted(range(1, 16), key=lambda d: abs(d - 8))
P1, PY, PN, PZ, P3, RC, RB, SZ, GB, GC, H1, H2, CM, CO, COUNT = 0, 1, 2, 3, 4, 5, 7, 8, 9, 13, 14, 15, 16, 17, 18


def dot(a, b, left, right):
    return lax.dot_general(a, b, (((left,), (right,)), ((), ())), preferred_element_type=F32)


def iota(shape, axis):
    return lax.broadcasted_iota(I32, shape, axis)


def two_parts(a):
    high = a.astype(BF16).astype(F32)
    return high, (a - high).astype(BF16).astype(F32)


def slopes(members, target):
    ratio = lambda d: d * lax.rsqrt(d * d + SMOOTH * SMOOTH)
    pair = [None] * MEMBERS
    for m in range(MEMBERS):
        for n in range(m + 1, MEMBERS):
            term = ratio(members[m] - members[n])
            pair[m] = term if pair[m] is None else pair[m] + term
            pair[n] = -term if pair[n] is None else pair[n] - term
    return [
        ratio(members[m] - target) * (1.0 / MEMBERS) - pair[m] * (1.0 / (MEMBERS * (MEMBERS - 1)))
        for m in range(MEMBERS)
    ]


def packed_slopes(packed):
    width = packed.shape[1]
    members = [packed[m * 16 : m * 16 + 16] for m in range(MEMBERS)]
    row = iota((16, width), 0)
    target = jnp.zeros((16, width), F32)
    for v in range(VB):
        at = target_row(v)
        target = jnp.where(row == v, packed[at : at + 1], target)
    return jnp.concatenate(slopes(members, target), axis=0)


def target_row(v):
    return (v % 8) * 16 + 13 + v // 8


def pooled_slopes(packed):
    area = packed[15:16]
    return packed_slopes(packed * (1.0 / jnp.where(area > 0.0, area, 1.0)))


def kernel(
    hid_in, tgt_in, area_in, rid_in, w_in, gh, gw,
    hid, tgt, area, rid, w, wp, tx, xs, psend, precv, gsend, grecv, sum_high, sum_low, mid_high, mid_low, spread,
    fine, middle, total, msend, yrecv, nrecv, zsend, zrecv,
    csend, crecv, own, bsend, brecv, strip, full, hsend, h1, h2send, h2, coarse_send, coarse_mine, tile_send, tile, grad, load, send, recv, relay,
):
    me, ce = lax.axis_index("mem"), lax.axis_index("cell")
    x, core = lax.div(me, 2), lax.rem(me, 2)
    z, y = lax.div(ce, 4), lax.rem(ce, 4)
    mem_peer = lambda d: {"mem": lax.rem(me + d, 8)}
    core_peer = {"mem": me + 1 - 2 * core}
    pair = lax.rem(z, 2)
    block_peer = lambda dx, dy, dz: {
        "mem": lax.rem(x + dx, 4) * 2 + core, "cell": (z + dz * (1 - 2 * pair)) * 4 + lax.rem(y + dy, 4)
    }
    y_peer = lambda d: {"cell": z * 4 + lax.rem(y + d, 4)}
    z_peer = lambda d: {"cell": lax.rem(z + d, 16) * 4 + y}
    near_peer = lambda d: {"cell": lax.rem(ce + 64 + d, 64)}

    def copy(source, landing, s, r, peer):
        return pltpu.make_async_remote_copy(
            src_ref=source, dst_ref=landing, send_sem=send.at[s], recv_sem=recv.at[r],
            device_id=peer, device_id_type=MESH,
        )

    def arrived(array, group):
        copy(array, array, group, group, core_peer).wait_recv()

    def sent(array, group):
        copy(array, array, group, group, core_peer).wait_send()

    def started(copies):
        for c in copies:
            c.start()
        return copies

    loads = [
        pltpu.make_async_copy(source, landing, load.at[i])
        for i, (source, landing) in enumerate([
            (w_in, w), (hid_in.at[0, pl.ds(0, 256)], hid.at[pl.ds(0, 256)]),
            (hid_in.at[0, pl.ds(256, 256)], hid.at[pl.ds(256, 256)]), (tgt_in, tgt), (area_in, area), (rid_in, rid),
        ])
    ]
    started(loads)
    barrier = pltpu.get_barrier_semaphore()
    peers = [mem_peer(d) for d in range(1, 8)] + [y_peer(d) for d in range(1, 4)]
    peers += [z_peer(1), z_peer(15)] + [near_peer(d) for d in NEAR]
    peers += [block_peer(0, dy, 1) for dy in (1, 2, 3)]
    for peer in peers:
        pl.semaphore_signal(barrier, inc=1, device_id=peer, device_id_type=MESH)

    row, col = iota((128, VARS), 0), iota((128, VARS), 1)
    block, place = lax.shift_right_logical(row, 4), row & 15
    pick = jnp.where((col == block * VB + place) & (place < VB), 1.0, 0.0).astype(BF16)
    loads[0].wait()
    wp[...] = dot(pick, w[...], 1, 0).astype(BF16)
    for i in range(2):
        loads[1 + i].wait()
        cells = slice(256 * i, 256 * i + 256)
        pred = dot(wp[...], hid[cells], 1, 1).astype(BF16)
        psend[:, :, cells] = pred.reshape(MEMBERS, 16, 256)

    def tell(step):
        for side in (1, -1):
            peer = z_peer(16 + side * 2**step)
            pl.semaphore_signal(relay.at[step], inc=1, device_id=peer, device_id_type=MESH)

    def hear(step):
        pl.semaphore_wait(relay.at[step], 2)

    pl.semaphore_wait(barrier, len(peers))
    started([
        copy(psend.at[lax.rem(me + d, 8)], precv.at[me], P1, P1, mem_peer(d))
        for d in MEM_STEPS
    ])
    tell(0)
    precv[pl.ds(me, 1)] = psend[pl.ds(me, 1)]

    for c in loads[3:]:
        c.wait()
    spot = jnp.where(place == 13, block, jnp.where((place == 14) & (block < VB - 8), block + 8, -1000))
    pick = jnp.where((spot >= 0) & (col == VB * me + spot), 1.0, 0.0).astype(BF16)
    tx[...] = dot(pick, tgt[...], 1, 0) + jnp.where(iota((128, 512), 0) == 15, 1.0, 0.0)

    ids = rid[...]
    mids, coarses = lax.shift_right_logical(ids, 4), lax.shift_right_logical(ids, 8)
    row = iota((8, 512), 0)
    key = jnp.where(row < 2, ids, jnp.where(row < 4, mids, coarses))
    ends = jnp.where(row % 2 == 0, key[:, 0:1], key[:, 511:512])
    label = jnp.where(row < 4, ends, row - 4)
    edge_high, edge_low = two_parts(jnp.where(key == label, area[...], 0.0))
    edge = jnp.concatenate([edge_high, edge_low], axis=0).astype(BF16)
    label_lane = jnp.where((iota((8, 128), 1) == 31) & (iota((8, 128), 0) < 4), label[:, 0:128].astype(F32), 0.0)

    turned = lambda a: jnp.transpose(jnp.broadcast_to(a, (128, 512)))
    ids_col = turned(ids.astype(F32))
    high_col, low_col = two_parts(turned(area[...]))
    for j in range(4):
        lanes = slice(128 * j, 128 * j + 128)
        same = ids_col == ids[:, lanes].astype(F32)
        sum_high[:, lanes] = jnp.where(same, high_col, 0.0).astype(BF16)
        sum_low[:, lanes] = jnp.where(same, low_col, 0.0).astype(BF16)
    first_id, last_id = ids[:, 0:1], ids[:, 511:512]
    first_mid, last_mid = mids[:, 0:1], mids[:, 511:512]
    same = lax.shift_right_logical(ids_col.astype(I32), 4) == iota((512, 128), 1) + first_mid
    mid_high[...] = jnp.where(same, high_col, 0.0).astype(BF16)
    mid_low[...] = jnp.where(same, low_col, 0.0).astype(BF16)
    inner = (mids == iota((128, 512), 0) + first_mid) & (mids != first_mid) & (mids != last_mid)
    spread[...] = jnp.where(inner, 1.0, 0.0).astype(BF16)

    hear(0)
    tell(1)
    arrived(precv.at[pl.ds(0, 7)], P1)
    values = (precv[...].reshape(128, 512).astype(F32) + tx[...]).astype(BF16)
    xs[...] = values
    pooled = dot(edge, values, 1, 1)
    msend[...] = pooled[0:8] + pooled[8:16] + label_lane
    started([
        copy(msend, nrecv.at[k], PN, PN, near_peer(d)) for k, d in enumerate(NEAR)
    ])

    started([
        copy(msend, yrecv.at[d - 1], PY, PY, y_peer(d)) for d in range(1, 4)
    ])
    hear(1)
    tell(2)
    kept = (iota((128, 128), 0) & 15) < VB
    fine[...] = dot(values, sum_high[...], 1, 0) + dot(values, sum_low[...], 1, 0)
    table = pooled_slopes(dot(values, mid_high[...], 1, 0) + dot(values, mid_low[...], 1, 0))
    table_high, table_low = two_parts(table)
    middle[...] = dot(table_high.astype(BF16), spread[...], 1, 0) + dot(table_low.astype(BF16), spread[...], 1, 0)

    def inner_slopes(j, carry):
        lanes = pl.ds(pl.multiple_of(j * 128, 128), 128)
        here = rid[:, lanes]
        alone = (here != first_id) & (here != last_id)
        slope = packed_slopes(xs[:, lanes].astype(F32)) + middle[:, lanes]
        total[:, lanes] = slope + jnp.where(alone, pooled_slopes(fine[:, lanes]), 0.0)
        return carry

    lax.fori_loop(0, 4, inner_slopes, 0)

    arrived(nrecv, PN)
    after_2, after, before, before_2 = [nrecv[k] for k in range(4)]
    edges = msend[...]

    def joined(at, others):
        line = edges[at : at + 1]
        for other in others:
            line = line + jnp.where(other[:, 31:32] == edges[at : at + 1, 31:32], other, 0.0)
        return line

    around = [before[3:4], before_2[3:4], after[2:3], after_2[2:3]]
    lines = [joined(0, [before[1:2]]), joined(1, [after[0:1]]), joined(2, around), joined(3, around)]
    ends = pooled_slopes(jnp.transpose(jnp.concatenate(lines + [jnp.zeros((124, 128), F32)], axis=0)))
    columns = [jnp.broadcast_to(ends[:, k : k + 1], (128, 128)) for k in range(4)]

    def all_slopes(j, carry):
        lanes = pl.ds(pl.multiple_of(j * 128, 128), 128)
        here = rid[:, lanes]
        mid = lax.shift_right_logical(here, 4)
        slope = total[:, lanes]
        slope = slope + jnp.where(here == first_id, columns[0], jnp.where(here == last_id, columns[1], 0.0))
        slope = slope + jnp.where(mid == first_mid, columns[2], jnp.where(mid == last_mid, columns[3], 0.0))
        part = jnp.where(kept, area[:, lanes] * slope, 0.0)
        gsend[:, :, lanes] = part.astype(BF16).reshape(MEMBERS, 16, 128)
        return carry

    lax.fori_loop(0, 4, all_slopes, 0)
    started([
        copy(gsend.at[lax.rem(me + d, 8)], grecv.at[me], P3, P3, mem_peer(d))
        for d in MEM_STEPS
    ])
    grecv[pl.ds(me, 1)] = gsend[pl.ds(me, 1)]

    hear(2)
    arrived(yrecv, PY)
    zsend[...] = (msend[...] + yrecv[0] + yrecv[1] + yrecv[2])[4:8]
    started([
        copy(zsend, zrecv.at[d - 1], PZ, PZ, z_peer(d)) for d in FAR_FIRST
    ])
    moment = dot(edge, hid[...], 1, 0)
    moment = (moment[0:8] + moment[8:16])[4:8]
    for j in range(8):
        at = 128 * ((j % 2) * 4 + j // 2)
        hsend[j] = moment[:, at : at + 128]
    started([
        copy(hsend.at[lax.rem(me + d, 8)], h1.at[me], H1, H1, mem_peer(d)) for d in MEM_STEPS
    ])
    h1[pl.ds(me, 1)] = hsend[pl.ds(me, 1)]
    arrived(grecv.at[pl.ds(0, 7)], P3)
    delta = grecv[...].reshape(128, 512)

    def weight_part(half, k):
        lanes = pl.ds(pl.multiple_of(half * 512 + 256 * k, 256), 256)
        product = dot(delta, hid[:, lanes], 1, 0)
        return [product[:, 128 * i : 128 * i + 128].reshape(8, 16, 128) for i in range(2)]

    cc = []
    for k in range(2):
        for i, part in enumerate(weight_part(1 - core, k)):
            csend[2 * k + i] = part.astype(BF16)
        cc += started([
            copy(csend.at[pl.ds(2 * k, 2)], crecv.at[pl.ds(2 * k, 2)], RC + k, RC + k, core_peer)
        ])
    for k in range(2):
        for i, part in enumerate(weight_part(core, k)):
            own[2 * k + i] = part
    arrived(h1.at[pl.ds(0, 7)], H1)
    moments = jnp.concatenate([h1[m] for m in range(8)], axis=0)
    h2send[...] = moments.astype(BF16)
    started([
        copy(h2send, h2.at[i], H2, H2, block_peer(0, dy, dz)) for i, (dy, dz) in enumerate(NEARBY)
    ])

    def block_copy(dx, dy, dz):
        slot = (dx * 4 + dy) * 2 + dz
        to = lax.rem(x + dx, 4), 2 * lax.rem(y + dy, 4) + pair + dz * (1 - 2 * pair)
        return copy(bsend.at[to], brecv.at[slot], RB, RB, block_peer(dx, dy, dz))

    for k in range(2):
        cc[k].wait_recv()
        for i in (2 * k, 2 * k + 1):
            both = own[i] + crecv[i].astype(F32)
            own[i] = both
            bsend[i] = both.astype(BF16)
        for i in (2 * k, 2 * k + 1):
            dx = lax.rem(i - x + 4, 4)
            for dy, dz in NEARBY:
                block_copy(dx, dy, dz).start()

            @pl.when(dx != 0)
            def _():
                block_copy(dx, 0, 0).start()

    arrived(zrecv, PZ)
    coarse_sum = zsend[...]
    for d in range(15):
        coarse_sum = coarse_sum + zrecv[d]
    coarse = jnp.transpose(jnp.concatenate([coarse_sum, jnp.zeros((124, 128), F32)], axis=0))
    inverse_area = ALL_CELLS / jnp.sum(coarse[15:16, 0:4], axis=1, keepdims=True)
    coarse_slope = jnp.where(kept, pooled_slopes(coarse), 0.0).reshape(MEMBERS, 16, 128)
    tile_send[...] = jnp.concatenate(
        [coarse_slope[m, :, 0:4] for m in range(MEMBERS)] + [jnp.zeros((16, 96), F32)], axis=1
    )
    coarse_send[...] = coarse_slope
    row_block = 2 * y + pair
    to_owner = [copy(tile_send, tile, CO, CO, mem_peer(d)) for d in MEM_STEPS]

    @pl.when(me == row_block)
    def _():
        started(to_owner)
        tile[...] = tile_send[...]

    arrived(h2, H2)
    for i in range(7):
        moments = moments + h2[i].astype(F32)

    @pl.when(me != row_block)
    def _():
        to_owner[0].wait_recv()

    piece = own[x, 2 * y + pair]
    share = tile[...]
    for i in range(32):
        piece = piece + share[:, i : i + 1] * moments[i : i + 1, :]
    arrived(brecv.at[pl.ds(1, 31)], RB)
    for dx, dy, dz in BLOCK:
        piece = piece + brecv[(dx * 4 + dy) * 2 + dz].astype(F32)
    piece = piece * inverse_area

    layer = lax.div(z, 2)
    strip[layer] = piece.astype(BF16)
    started([
        copy(
            strip.at[layer], strip.at[layer], SZ, SZ,
            {"cell": (lax.rem(layer + d, 8) * 2 + pair) * 4 + y},
        )
        for d in (4, 3, 5, 2, 6, 1, 7)
    ])
    started([
        copy(coarse_send.at[lax.rem(me + d, 8)], coarse_mine.at[me], CM, CM, mem_peer(d))
        for d in MEM_STEPS
    ])
    coarse_mine[pl.ds(me, 1)] = coarse_send[pl.ds(me, 1)]
    sent(psend.at[pl.ds(0, 7)], P1)
    sent(nrecv, PN)
    sent(yrecv, PY)
    sent(gsend.at[pl.ds(0, 7)], P3)
    sent(zrecv, PZ)
    sent(h1.at[pl.ds(0, 7)], H1)
    sent(h2, H2)
    sent(brecv.at[pl.ds(1, 31)], RB)
    for c in cc:
        c.wait_send()

    @pl.when(me == row_block)
    def _():
        sent(coarse_send.at[pl.ds(0, 7)], CO)

    arrived(coarse_mine.at[pl.ds(0, 7)], CM)
    sent(coarse_send.at[pl.ds(0, 7)], CM)
    columns = [jnp.broadcast_to(coarse_mine[...].reshape(128, 128)[:, k : k + 1], (128, 128)) for k in range(4)]

    def gradient(j, carry):
        lanes = pl.ds(pl.multiple_of(j * 128, 128), 128)
        key = lax.shift_right_logical(rid[:, lanes], 8)
        slope = jnp.zeros((128, 128), F32)
        for k in range(4):
            slope = jnp.where(key == k, columns[k], slope)
        part = grecv[:, :, lanes].reshape(128, 128).astype(F32)
        grad[:, lanes] = ((part + area[:, lanes] * slope) * inverse_area).astype(BF16)
        return carry

    lax.fori_loop(0, 4, gradient, 0)
    arrived(strip.at[pl.ds(0, 7)], SZ)
    piece = strip[0].astype(F32)
    for k in range(1, 8):
        piece = piece + strip[k].astype(F32)
    chunk = core * 4 + x
    full[chunk, row_block] = piece.astype(BF16)

    spot = full.at[chunk, row_block]
    started([copy(spot, spot, GB, GB + at[0], block_peer(*at)) for i, at in enumerate(BLOCK)])
    gh[0] = dot(grad[...], wp[...], 0, 0).astype(BF16)
    sent(strip.at[pl.ds(0, 7)], SZ)
    for dx in (0, 1, 3, 2):
        arrived(full.at[0, pl.ds(0, 8 if dx else 7)], GB + dx)
        spot = full.at[core * 4 + lax.rem(x - dx + 4, 4)]
        started([copy(spot, spot, GC, GC, core_peer)])
    sent(brecv.at[pl.ds(1, 31)], GB)
    arrived(full.at[pl.ds(0, 4)], GC)

    square = jnp.zeros((16, 128), F32)
    for k in range(8):
        part = full[k].astype(F32)
        square = square + jnp.sum(part * part, axis=0)
    mean_square = jnp.sum(square, keepdims=True) * (1.0 / (VARS * 1024))
    scale = lax.rsqrt(mean_square + 1e-06)
    for k in range(8):
        for j in range(8):
            rows = min(VB, VARS - VB * j)
            gw[VB * j : VB * j + rows, 128 * k : 128 * k + 128] = (full[k, j].astype(F32) * scale)[0:rows]

    sent(full.at[pl.ds(0, 4)], GC)


def write_out(gh, gw, gh_out, gw_out, done):
    copies = [pltpu.make_async_copy(gh, gh_out, done.at[0]), pltpu.make_async_copy(gw, gw_out, done.at[1])]
    for c in copies:
        c.start()
    for c in copies:
        c.wait()


def local(hidden_states, targets, cell_area, region_ids, decoder_weight):
    anywhere = pl.BlockSpec(memory_space=pl.ANY)
    vmem = pl.BlockSpec(memory_space=pltpu.VMEM)
    scratch = [
        ((512, 1024), BF16), ((VARS, 512), BF16), ((1, 512), F32), ((1, 512), I32), ((VARS, 1024), BF16),
        ((128, 1024), BF16), ((128, 512), F32), ((128, 512), BF16),
        ((8, 16, 512), BF16), ((8, 16, 512), BF16), ((8, 16, 512), BF16), ((8, 16, 512), BF16),
        ((512, 512), BF16), ((512, 512), BF16), ((512, 128), BF16), ((512, 128), BF16), ((128, 512), BF16),
        ((128, 512), F32), ((128, 512), F32), ((128, 512), F32),
        ((8, 128), F32), ((3, 8, 128), F32), ((4, 8, 128), F32), ((4, 128), F32), ((15, 4, 128), F32),
        ((4, 8, 16, 128), BF16), ((4, 8, 16, 128), BF16), ((4, 8, 16, 128), F32), ((4, 8, 16, 128), BF16),
        ((32, 16, 128), BF16), ((8, 16, 128), BF16), ((8, 8, 16, 128), BF16),
        ((8, 4, 128), F32), ((8, 4, 128), F32), ((32, 128), BF16), ((7, 32, 128), BF16),
        ((8, 16, 128), F32), ((8, 16, 128), F32), ((16, 128), F32), ((16, 128), F32), ((128, 512), BF16),
    ]
    arguments = (
        hidden_states, targets, cell_area.reshape(1, -1), region_ids.reshape(1, -1), decoder_weight.T
    )
    results = (
        jax.ShapeDtypeStruct(hidden_states.shape, BF16),
        jax.ShapeDtypeStruct((VARS, 1024), F32),
    )
    grad_hidden, grad_weight = pl.pallas_call(
        kernel,
        out_shape=results,
        in_specs=[anywhere] * 5,
        out_specs=(vmem, vmem),
        scratch_shapes=[pltpu.VMEM(s, t) for s, t in scratch]
        + [pltpu.SemaphoreType.DMA((n,)) for n in (6, COUNT, COUNT)]
        + [pltpu.SemaphoreType.REGULAR((3,))],
        compiler_params=pltpu.CompilerParams(
            collective_id=0, has_side_effects=True, vmem_limit_bytes=VMEM_LIMIT
        ),
    )(*[pltpu.with_memory_space_constraint(a, pltpu.HBM) for a in arguments])
    grad_hidden, grad_weight = pl.pallas_call(
        write_out,
        out_shape=results,
        in_specs=[vmem] * 2,
        out_specs=(anywhere, anywhere),
        scratch_shapes=[pltpu.SemaphoreType.DMA((2,))],
    )(*[pltpu.with_memory_space_constraint(a, pltpu.VMEM) for a in (grad_hidden, grad_weight)])
    return grad_hidden, grad_weight.T


def solution(mesh):
    in_specs = (P("mem", "cell", None), P(None, "cell"), P("cell"), P("cell"), P())
    out_specs = (P("mem", "cell", None), P())
    return jax.shard_map(local, mesh=mesh, in_specs=in_specs, out_specs=out_specs, check_vma=False)
```

```python
import functools

import jax
import jax.numpy as jnp
from jax import lax
from jax.experimental import pallas as pl
from jax.experimental.pallas import tpu as pltpu
from jax.sharding import PartitionSpec as P

LOGICAL = pl.DeviceIdType.LOGICAL
F32, BF16, I32 = jnp.float32, jnp.bfloat16, jnp.int32
SMOOTH = 0.1
MEMBERS = 8
VARS = 100
VB = 13
ALL_CELLS = 32768
VMEM_LIMIT = 32 * 1024 * 1024
NEAR = (-2, -1, 1, 2)
BLOCK = [(dx, dy, dz) for dx in (2, 1, 3, 0) for dy in (2, 1, 3, 0) for dz in (1, 0) if dx or dy or dz]
NEARBY = [(dy, dz) for dy in (2, 1, 3, 0) for dz in (1, 0) if dy or dz]
MEM_STEPS = (4, 3, 5, 2, 6, 1, 7)
FAR_FIRST = sorted(range(1, 16), key=lambda d: abs(d - 8))
P1, PY, PN, PZ, P3, RC, RB, SZ, GB, GC, H1, H2, CM, CO, COUNT = 0, 1, 2, 3, 4, 5, 7, 8, 9, 13, 14, 15, 16, 17, 18


def dot(a, b, left, right):
    return lax.dot_general(a, b, (((left,), (right,)), ((), ())), preferred_element_type=F32)


def iota(shape, axis):
    return lax.broadcasted_iota(I32, shape, axis)


def two_parts(a):
    high = a.astype(BF16).astype(F32)
    return high, (a - high).astype(BF16).astype(F32)


def slopes(members, target):
    ratio = lambda d: d * lax.rsqrt(d * d + SMOOTH * SMOOTH)
    pair = [None] * MEMBERS
    for m in range(MEMBERS):
        for n in range(m + 1, MEMBERS):
            term = ratio(members[m] - members[n])
            pair[m] = term if pair[m] is None else pair[m] + term
            pair[n] = -term if pair[n] is None else pair[n] - term
    return [
        ratio(members[m] - target) * (1.0 / MEMBERS) - pair[m] * (1.0 / (MEMBERS * (MEMBERS - 1)))
        for m in range(MEMBERS)
    ]


def packed_slopes(packed):
    width = packed.shape[1]
    members = [packed[m * 16 : m * 16 + 16] for m in range(MEMBERS)]
    row = iota((16, width), 0)
    target = jnp.zeros((16, width), F32)
    for v in range(VB):
        at = target_row(v)
        target = jnp.where(row == v, packed[at : at + 1], target)
    return jnp.concatenate(slopes(members, target), axis=0)


def target_row(v):
    return (v % 8) * 16 + 13 + v // 8


def pooled_slopes(packed):
    area = packed[15:16]
    return packed_slopes(packed * (1.0 / jnp.where(area > 0.0, area, 1.0)))


def kernel(
    hid_in, tgt_in, area_in, rid_in, w_in, gh, gw,
    hid, tgt, area, rid, w, wp, tx, xs, psend, precv, gsend, grecv, sum_high, sum_low, mid_high, mid_low, spread,
    fine, middle, total, msend, yrecv, nrecv, zsend, zrecv,
    csend, crecv, own, bsend, brecv, strip, full, hsend, h1, h2send, h2, coarse_send, coarse_mine, tile_send, tile, grad, load, send, recv, relay,
):
    me, ce = lax.axis_index("mem"), lax.axis_index("cell")
    x, core = lax.div(me, 2), lax.rem(me, 2)
    z, y = lax.div(ce, 4), lax.rem(ce, 4)
    pair = lax.rem(z, 2)
    here = ce * 8
    xs_at = [lax.rem(x + d, 4) for d in range(4)]
    ys_at = [lax.rem(y + d, 4) for d in range(4)]
    mems = [lax.rem(me + d, 8) for d in range(8)]
    pairs = [pair, 1 - pair]
    layers = [z * 32, (z + 1 - 2 * pair) * 32]
    rows = [[layer + 8 * at + core for at in ys_at] for layer in layers]
    mem_peer = lambda d: here + mems[d]
    core_peer = here + me + 1 - 2 * core
    block_peer = lambda dx, dy, dz: rows[dz][dy] + 2 * xs_at[dx]
    y_peer = lambda d: layers[0] + 8 * ys_at[d] + me
    z_peer = lambda d: lax.rem(z + d, 16) * 32 + (8 * y + me)
    near_peer = lambda d: lax.rem(ce + 64 + d, 64) * 8 + me

    def copy(source, landing, s, r, peer):
        return pltpu.make_async_remote_copy(
            src_ref=source, dst_ref=landing, send_sem=send.at[s], recv_sem=recv.at[r],
            device_id=peer, device_id_type=LOGICAL,
        )

    def arrived(array, group):
        copy(array, array, group, group, core_peer).wait_recv()

    def sent(array, group):
        copy(array, array, group, group, core_peer).wait_send()

    def started(copies):
        for c in copies:
            c.start()
        return copies

    loads = [
        pltpu.make_async_copy(source, landing, load.at[i])
        for i, (source, landing) in enumerate([
            (w_in, w), (hid_in.at[0, pl.ds(0, 256)], hid.at[pl.ds(0, 256)]),
            (hid_in.at[0, pl.ds(256, 256)], hid.at[pl.ds(256, 256)]), (tgt_in, tgt), (area_in, area), (rid_in, rid),
        ])
    ]
    started(loads)
    barrier = pltpu.get_barrier_semaphore()
    peers = [mem_peer(d) for d in range(1, 8)] + [y_peer(d) for d in range(1, 4)]
    peers += [z_peer(1), z_peer(15)] + [near_peer(d) for d in NEAR]
    peers += [block_peer(0, dy, 1) for dy in (1, 2, 3)]
    for peer in peers:
        pl.semaphore_signal(barrier, inc=1, device_id=peer, device_id_type=LOGICAL)

    row, col = iota((128, VARS), 0), iota((128, VARS), 1)
    block, place = lax.shift_right_logical(row, 4), row & 15
    pick = jnp.where((col == block * VB + place) & (place < VB), 1.0, 0.0).astype(BF16)
    loads[0].wait()
    wp[...] = dot(pick, w[...], 1, 0).astype(BF16)
    for i in range(2):
        loads[1 + i].wait()
        cells = slice(256 * i, 256 * i + 256)
        pred = dot(wp[...], hid[cells], 1, 1).astype(BF16)
        psend[:, :, cells] = pred.reshape(MEMBERS, 16, 256)

    def tell(step):
        for side in (1, -1):
            peer = z_peer(16 + side * 2**step)
            pl.semaphore_signal(relay.at[step], inc=1, device_id=peer, device_id_type=LOGICAL)

    def hear(step):
        pl.semaphore_wait(relay.at[step], 2)

    pl.semaphore_wait(barrier, len(peers))
    started([
        copy(psend.at[mems[d]], precv.at[me], P1, P1, mem_peer(d))
        for d in MEM_STEPS
    ])
    tell(0)
    precv[pl.ds(me, 1)] = psend[pl.ds(me, 1)]

    for c in loads[3:]:
        c.wait()
    spot = jnp.where(place == 13, block, jnp.where((place == 14) & (block < VB - 8), block + 8, -1000))
    pick = jnp.where((spot >= 0) & (col == VB * me + spot), 1.0, 0.0).astype(BF16)
    tx[...] = dot(pick, tgt[...], 1, 0) + jnp.where(iota((128, 512), 0) == 15, 1.0, 0.0)

    ids = rid[...]
    mids, coarses = lax.shift_right_logical(ids, 4), lax.shift_right_logical(ids, 8)
    row = iota((8, 512), 0)
    key = jnp.where(row < 2, ids, jnp.where(row < 4, mids, coarses))
    ends = jnp.where(row % 2 == 0, key[:, 0:1], key[:, 511:512])
    label = jnp.where(row < 4, ends, row - 4)
    edge_high, edge_low = two_parts(jnp.where(key == label, area[...], 0.0))
    edge = jnp.concatenate([edge_high, edge_low], axis=0).astype(BF16)
    label_lane = jnp.where((iota((8, 128), 1) == 31) & (iota((8, 128), 0) < 4), label[:, 0:128].astype(F32), 0.0)

    turned = lambda a: jnp.transpose(jnp.broadcast_to(a, (128, 512)))
    ids_col = turned(ids.astype(F32))
    high_col, low_col = two_parts(turned(area[...]))
    for j in range(4):
        lanes = slice(128 * j, 128 * j + 128)
        same = ids_col == ids[:, lanes].astype(F32)
        sum_high[:, lanes] = jnp.where(same, high_col, 0.0).astype(BF16)
        sum_low[:, lanes] = jnp.where(same, low_col, 0.0).astype(BF16)
    first_id, last_id = ids[:, 0:1], ids[:, 511:512]
    first_mid, last_mid = mids[:, 0:1], mids[:, 511:512]
    same = lax.shift_right_logical(ids_col.astype(I32), 4) == iota((512, 128), 1) + first_mid
    mid_high[...] = jnp.where(same, high_col, 0.0).astype(BF16)
    mid_low[...] = jnp.where(same, low_col, 0.0).astype(BF16)
    inner = (mids == iota((128, 512), 0) + first_mid) & (mids != first_mid) & (mids != last_mid)
    spread[...] = jnp.where(inner, 1.0, 0.0).astype(BF16)

    hear(0)
    tell(1)
    arrived(precv.at[pl.ds(0, 7)], P1)
    values = (precv[...].reshape(128, 512).astype(F32) + tx[...]).astype(BF16)
    xs[...] = values
    pooled = dot(edge, values, 1, 1)
    msend[...] = pooled[0:8] + pooled[8:16] + label_lane
    started([
        copy(msend, nrecv.at[k], PN, PN, near_peer(d)) for k, d in enumerate(NEAR)
    ])

    started([
        copy(msend, yrecv.at[d - 1], PY, PY, y_peer(d)) for d in range(1, 4)
    ])
    hear(1)
    tell(2)
    kept = (iota((128, 128), 0) & 15) < VB
    fine[...] = dot(values, sum_high[...], 1, 0) + dot(values, sum_low[...], 1, 0)
    table = pooled_slopes(dot(values, mid_high[...], 1, 0) + dot(values, mid_low[...], 1, 0))
    table_high, table_low = two_parts(table)
    middle[...] = dot(table_high.astype(BF16), spread[...], 1, 0) + dot(table_low.astype(BF16), spread[...], 1, 0)

    def inner_slopes(j, carry):
        lanes = pl.ds(pl.multiple_of(j * 128, 128), 128)
        here = rid[:, lanes]
        alone = (here != first_id) & (here != last_id)
        slope = packed_slopes(xs[:, lanes].astype(F32)) + middle[:, lanes]
        total[:, lanes] = slope + jnp.where(alone, pooled_slopes(fine[:, lanes]), 0.0)
        return carry

    lax.fori_loop(0, 4, inner_slopes, 0)

    arrived(nrecv, PN)
    after_2, after, before, before_2 = [nrecv[k] for k in range(4)]
    edges = msend[...]

    def joined(at, others):
        line = edges[at : at + 1]
        for other in others:
            line = line + jnp.where(other[:, 31:32] == edges[at : at + 1, 31:32], other, 0.0)
        return line

    around = [before[3:4], before_2[3:4], after[2:3], after_2[2:3]]
    lines = [joined(0, [before[1:2]]), joined(1, [after[0:1]]), joined(2, around), joined(3, around)]
    ends = pooled_slopes(jnp.transpose(jnp.concatenate(lines + [jnp.zeros((124, 128), F32)], axis=0)))
    columns = [jnp.broadcast_to(ends[:, k : k + 1], (128, 128)) for k in range(4)]

    def all_slopes(j, carry):
        lanes = pl.ds(pl.multiple_of(j * 128, 128), 128)
        here = rid[:, lanes]
        mid = lax.shift_right_logical(here, 4)
        slope = total[:, lanes]
        slope = slope + jnp.where(here == first_id, columns[0], jnp.where(here == last_id, columns[1], 0.0))
        slope = slope + jnp.where(mid == first_mid, columns[2], jnp.where(mid == last_mid, columns[3], 0.0))
        part = jnp.where(kept, area[:, lanes] * slope, 0.0)
        gsend[:, :, lanes] = part.astype(BF16).reshape(MEMBERS, 16, 128)
        return carry

    lax.fori_loop(0, 4, all_slopes, 0)
    started([
        copy(gsend.at[mems[d]], grecv.at[me], P3, P3, mem_peer(d))
        for d in MEM_STEPS
    ])
    grecv[pl.ds(me, 1)] = gsend[pl.ds(me, 1)]

    hear(2)
    arrived(yrecv, PY)
    zsend[...] = (msend[...] + yrecv[0] + yrecv[1] + yrecv[2])[4:8]
    started([
        copy(zsend, zrecv.at[d - 1], PZ, PZ, z_peer(d)) for d in FAR_FIRST
    ])
    moment = dot(edge, hid[...], 1, 0)
    moment = (moment[0:8] + moment[8:16])[4:8]
    for j in range(8):
        at = 128 * ((j % 2) * 4 + j // 2)
        hsend[j] = moment[:, at : at + 128]
    started([
        copy(hsend.at[mems[d]], h1.at[me], H1, H1, mem_peer(d)) for d in MEM_STEPS
    ])
    h1[pl.ds(me, 1)] = hsend[pl.ds(me, 1)]
    arrived(grecv.at[pl.ds(0, 7)], P3)
    delta = grecv[...].reshape(128, 512)

    def weight_part(half, k):
        lanes = pl.ds(pl.multiple_of(half * 512 + 256 * k, 256), 256)
        product = dot(delta, hid[:, lanes], 1, 0)
        return [product[:, 128 * i : 128 * i + 128].reshape(8, 16, 128) for i in range(2)]

    cc = []
    for k in range(2):
        for i, part in enumerate(weight_part(1 - core, k)):
            csend[2 * k + i] = part.astype(BF16)
        cc += started([
            copy(csend.at[pl.ds(2 * k, 2)], crecv.at[pl.ds(2 * k, 2)], RC + k, RC + k, core_peer)
        ])
    for k in range(2):
        for i, part in enumerate(weight_part(core, k)):
            own[2 * k + i] = part
    arrived(h1.at[pl.ds(0, 7)], H1)
    moments = jnp.concatenate([h1[m] for m in range(8)], axis=0)
    h2send[...] = moments.astype(BF16)
    started([
        copy(h2send, h2.at[i], H2, H2, block_peer(0, dy, dz)) for i, (dy, dz) in enumerate(NEARBY)
    ])

    def block_copy(i, dx, dy, dz):
        slot = dx * 8 + dy * 2 + dz
        peer = rows[dz][dy] + 2 * i
        return copy(bsend.at[i, 2 * ys_at[dy] + pairs[dz]], brecv.at[slot], RB, RB, peer)

    for k in range(2):
        cc[k].wait_recv()
        for i in (2 * k, 2 * k + 1):
            both = own[i] + crecv[i].astype(F32)
            own[i] = both
            bsend[i] = both.astype(BF16)
        for i in (2 * k, 2 * k + 1):
            dx = lax.rem(i - x + 4, 4)
            for dy, dz in NEARBY:
                block_copy(i, dx, dy, dz).start()

            @pl.when(dx != 0)
            def _():
                block_copy(i, dx, 0, 0).start()

    arrived(zrecv, PZ)
    coarse_sum = zsend[...]
    for d in range(15):
        coarse_sum = coarse_sum + zrecv[d]
    coarse = jnp.transpose(jnp.concatenate([coarse_sum, jnp.zeros((124, 128), F32)], axis=0))
    inverse_area = ALL_CELLS / jnp.sum(coarse[15:16, 0:4], axis=1, keepdims=True)
    coarse_slope = jnp.where(kept, pooled_slopes(coarse), 0.0).reshape(MEMBERS, 16, 128)
    tile_send[...] = jnp.concatenate(
        [coarse_slope[m, :, 0:4] for m in range(MEMBERS)] + [jnp.zeros((16, 96), F32)], axis=1
    )
    coarse_send[...] = coarse_slope
    row_block = 2 * y + pair
    to_owner = [copy(tile_send, tile, CO, CO, mem_peer(d)) for d in MEM_STEPS]

    @pl.when(me == row_block)
    def _():
        started(to_owner)
        tile[...] = tile_send[...]

    arrived(h2, H2)
    for i in range(7):
        moments = moments + h2[i].astype(F32)

    @pl.when(me != row_block)
    def _():
        to_owner[0].wait_recv()

    piece = own[x, 2 * y + pair]
    share = tile[...]
    for i in range(32):
        piece = piece + share[:, i : i + 1] * moments[i : i + 1, :]
    arrived(brecv.at[pl.ds(1, 31)], RB)
    for dx, dy, dz in BLOCK:
        piece = piece + brecv[(dx * 4 + dy) * 2 + dz].astype(F32)
    piece = piece * inverse_area

    layer = lax.div(z, 2)
    strip[layer] = piece.astype(BF16)
    started([
        copy(
            strip.at[layer], strip.at[layer], SZ, SZ,
            z_peer(2 * d),
        )
        for d in (4, 3, 5, 2, 6, 1, 7)
    ])
    started([
        copy(coarse_send.at[mems[d]], coarse_mine.at[me], CM, CM, mem_peer(d))
        for d in MEM_STEPS
    ])
    coarse_mine[pl.ds(me, 1)] = coarse_send[pl.ds(me, 1)]
    sent(psend.at[pl.ds(0, 7)], P1)
    sent(nrecv, PN)
    sent(yrecv, PY)
    sent(gsend.at[pl.ds(0, 7)], P3)
    sent(zrecv, PZ)
    sent(h1.at[pl.ds(0, 7)], H1)
    sent(h2, H2)
    sent(brecv.at[pl.ds(1, 31)], RB)
    for c in cc:
        c.wait_send()

    @pl.when(me == row_block)
    def _():
        sent(coarse_send.at[pl.ds(0, 7)], CO)

    arrived(coarse_mine.at[pl.ds(0, 7)], CM)
    sent(coarse_send.at[pl.ds(0, 7)], CM)
    columns = [jnp.broadcast_to(coarse_mine[...].reshape(128, 128)[:, k : k + 1], (128, 128)) for k in range(4)]

    def gradient(j, carry):
        lanes = pl.ds(pl.multiple_of(j * 128, 128), 128)
        key = lax.shift_right_logical(rid[:, lanes], 8)
        slope = jnp.zeros((128, 128), F32)
        for k in range(4):
            slope = jnp.where(key == k, columns[k], slope)
        part = grecv[:, :, lanes].reshape(128, 128).astype(F32)
        grad[:, lanes] = ((part + area[:, lanes] * slope) * inverse_area).astype(BF16)
        return carry

    lax.fori_loop(0, 4, gradient, 0)
    arrived(strip.at[pl.ds(0, 7)], SZ)
    piece = strip[0].astype(F32)
    for k in range(1, 8):
        piece = piece + strip[k].astype(F32)
    chunk = core * 4 + x
    full[chunk, row_block] = piece.astype(BF16)

    spot = full.at[chunk, row_block]
    started([copy(spot, spot, GB, GB + at[0], block_peer(*at)) for i, at in enumerate(BLOCK)])
    gh[0] = dot(grad[...], wp[...], 0, 0).astype(BF16)
    sent(strip.at[pl.ds(0, 7)], SZ)
    for dx in (0, 1, 3, 2):
        arrived(full.at[0, pl.ds(0, 8 if dx else 7)], GB + dx)
        spot = full.at[core * 4 + xs_at[(4 - dx) % 4]]
        started([copy(spot, spot, GC, GC, core_peer)])
    sent(brecv.at[pl.ds(1, 31)], GB)
    arrived(full.at[pl.ds(0, 4)], GC)

    square = jnp.zeros((16, 128), F32)
    for k in range(8):
        part = full[k].astype(F32)
        square = square + jnp.sum(part * part, axis=0)
    mean_square = jnp.sum(square, keepdims=True) * (1.0 / (VARS * 1024))
    scale = lax.rsqrt(mean_square + 1e-06)
    for k in range(8):
        for j in range(8):
            rows = min(VB, VARS - VB * j)
            gw[VB * j : VB * j + rows, 128 * k : 128 * k + 128] = (full[k, j].astype(F32) * scale)[0:rows]

    sent(full.at[pl.ds(0, 4)], GC)


def write_out(gh, gw, gh_out, gw_out, done):
    copies = [pltpu.make_async_copy(gh, gh_out, done.at[0]), pltpu.make_async_copy(gw, gw_out, done.at[1])]
    for c in copies:
        c.start()
    for c in copies:
        c.wait()


def local(hidden_states, targets, cell_area, region_ids, decoder_weight):
    anywhere = pl.BlockSpec(memory_space=pl.ANY)
    vmem = pl.BlockSpec(memory_space=pltpu.VMEM)
    scratch = [
        ((512, 1024), BF16), ((VARS, 512), BF16), ((1, 512), F32), ((1, 512), I32), ((VARS, 1024), BF16),
        ((128, 1024), BF16), ((128, 512), F32), ((128, 512), BF16),
        ((8, 16, 512), BF16), ((8, 16, 512), BF16), ((8, 16, 512), BF16), ((8, 16, 512), BF16),
        ((512, 512), BF16), ((512, 512), BF16), ((512, 128), BF16), ((512, 128), BF16), ((128, 512), BF16),
        ((128, 512), F32), ((128, 512), F32), ((128, 512), F32),
        ((8, 128), F32), ((3, 8, 128), F32), ((4, 8, 128), F32), ((4, 128), F32), ((15, 4, 128), F32),
        ((4, 8, 16, 128), BF16), ((4, 8, 16, 128), BF16), ((4, 8, 16, 128), F32), ((4, 8, 16, 128), BF16),
        ((32, 16, 128), BF16), ((8, 16, 128), BF16), ((8, 8, 16, 128), BF16),
        ((8, 4, 128), F32), ((8, 4, 128), F32), ((32, 128), BF16), ((7, 32, 128), BF16),
        ((8, 16, 128), F32), ((8, 16, 128), F32), ((16, 128), F32), ((16, 128), F32), ((128, 512), BF16),
    ]
    arguments = (
        hidden_states, targets, cell_area.reshape(1, -1), region_ids.reshape(1, -1), decoder_weight.T
    )
    results = (
        jax.ShapeDtypeStruct(hidden_states.shape, BF16),
        jax.ShapeDtypeStruct((VARS, 1024), F32),
    )
    grad_hidden, grad_weight = pl.pallas_call(
        kernel,
        out_shape=results,
        in_specs=[anywhere] * 5,
        out_specs=(vmem, vmem),
        scratch_shapes=[pltpu.VMEM(s, t) for s, t in scratch]
        + [pltpu.SemaphoreType.DMA((n,)) for n in (6, COUNT, COUNT)]
        + [pltpu.SemaphoreType.REGULAR((3,))],
        compiler_params=pltpu.CompilerParams(
            collective_id=0, has_side_effects=True, vmem_limit_bytes=VMEM_LIMIT
        ),
    )(*[pltpu.with_memory_space_constraint(a, pltpu.HBM) for a in arguments])
    grad_hidden, grad_weight = pl.pallas_call(
        write_out,
        out_shape=results,
        in_specs=[vmem] * 2,
        out_specs=(anywhere, anywhere),
        scratch_shapes=[pltpu.SemaphoreType.DMA((2,))],
    )(*[pltpu.with_memory_space_constraint(a, pltpu.VMEM) for a in (grad_hidden, grad_weight)])
    return grad_hidden, grad_weight.T


def solution(mesh):
    in_specs = (P("mem", "cell", None), P(None, "cell"), P("cell"), P("cell"), P())
    out_specs = (P("mem", "cell", None), P())
    return jax.shard_map(local, mesh=mesh, in_specs=in_specs, out_specs=out_specs, check_vma=False)
```

```python
import functools

import jax
import jax.numpy as jnp
from jax import lax
from jax.experimental import pallas as pl
from jax.experimental.pallas import tpu as pltpu
from jax.sharding import PartitionSpec as P

LOGICAL = pl.DeviceIdType.LOGICAL
F32, BF16, I32 = jnp.float32, jnp.bfloat16, jnp.int32
SMOOTH = 0.1
MEMBERS = 8
VARS = 100
VB = 13
ALL_CELLS = 32768
VMEM_LIMIT = 32 * 1024 * 1024
NEAR = (-2, -1, 1, 2)
BLOCK = [(dx, dy, dz) for dx in (2, 1, 3, 0) for dy in (2, 1, 3, 0) for dz in (1, 0) if dx or dy or dz]
NEARBY = [(dy, dz) for dy in (2, 1, 3, 0) for dz in (1, 0) if dy or dz]
MEM_STEPS = (4, 3, 5, 2, 6, 1, 7)
FAR_FIRST = sorted(range(1, 16), key=lambda d: abs(d - 8))
P1, PY, PN, PZ, P3, RC, RB, SZ, GB, GC, H1, H2, CM, CO, COUNT = 0, 1, 2, 3, 4, 5, 7, 8, 9, 13, 14, 15, 16, 17, 18


def dot(a, b, left, right):
    return lax.dot_general(a, b, (((left,), (right,)), ((), ())), preferred_element_type=F32)


def iota(shape, axis):
    return lax.broadcasted_iota(I32, shape, axis)


def two_parts(a):
    high = a.astype(BF16).astype(F32)
    return high, (a - high).astype(BF16).astype(F32)


def slopes(members, target):
    ratio = lambda d: d * lax.rsqrt(d * d + SMOOTH * SMOOTH)
    pair = [None] * MEMBERS
    for m in range(MEMBERS):
        for n in range(m + 1, MEMBERS):
            term = ratio(members[m] - members[n])
            pair[m] = term if pair[m] is None else pair[m] + term
            pair[n] = -term if pair[n] is None else pair[n] - term
    return [
        ratio(members[m] - target) * (1.0 / MEMBERS) - pair[m] * (1.0 / (MEMBERS * (MEMBERS - 1)))
        for m in range(MEMBERS)
    ]


def packed_slopes(packed):
    width = packed.shape[1]
    members = [packed[m * 16 : m * 16 + 16] for m in range(MEMBERS)]
    row = iota((16, width), 0)
    target = jnp.zeros((16, width), F32)
    for v in range(VB):
        at = target_row(v)
        target = jnp.where(row == v, packed[at : at + 1], target)
    return jnp.concatenate(slopes(members, target), axis=0)


def target_row(v):
    return (v % 8) * 16 + 13 + v // 8


def pooled_slopes(packed):
    area = packed[15:16]
    return packed_slopes(packed * (1.0 / jnp.where(area > 0.0, area, 1.0)))


def kernel(
    hid_in, tgt_in, area_in, rid_in, w_in, gh, gw,
    hid, tgt, area, rid, w, wp, tx, xs, psend, precv, gsend, grecv, sum_high, sum_low, mid_high, mid_low, spread,
    fine, middle, total, msend, yrecv, nrecv, zsend, zrecv,
    csend, crecv, own, bsend, brecv, strip, full, hsend, h1, h2send, h2, coarse_send, coarse_mine, tile_send, tile, grad, load, send, recv, relay,
):
    me, ce = lax.axis_index("mem"), lax.axis_index("cell")
    x, core = lax.div(me, 2), lax.rem(me, 2)
    z, y = lax.div(ce, 4), lax.rem(ce, 4)
    pair = lax.rem(z, 2)
    here = ce * 8
    xs_at = [lax.rem(x + d, 4) for d in range(4)]
    ys_at = [lax.rem(y + d, 4) for d in range(4)]
    mems = [lax.rem(me + d, 8) for d in range(8)]
    pairs = [pair, 1 - pair]
    layers = [z * 32, (z + 1 - 2 * pair) * 32]
    rows = [[layer + 8 * at + core for at in ys_at] for layer in layers]
    mem_peer = lambda d: here + mems[d]
    core_peer = here + me + 1 - 2 * core
    block_peer = lambda dx, dy, dz: rows[dz][dy] + 2 * xs_at[dx]
    y_peer = lambda d: layers[0] + 8 * ys_at[d] + me
    z_peer = lambda d: lax.rem(z + d, 16) * 32 + (8 * y + me)
    near_peer = lambda d: lax.rem(ce + 64 + d, 64) * 8 + me

    def copy(source, landing, s, r, peer):
        return pltpu.make_async_remote_copy(
            src_ref=source, dst_ref=landing, send_sem=send.at[s], recv_sem=recv.at[r],
            device_id=peer, device_id_type=LOGICAL,
        )

    def arrived(array, group):
        copy(array, array, group, group, core_peer).wait_recv()

    def sent(array, group):
        copy(array, array, group, group, core_peer).wait_send()

    def started(copies):
        for c in copies:
            c.start()
        return copies

    loads = [
        pltpu.make_async_copy(source, landing, load.at[i])
        for i, (source, landing) in enumerate([
            (w_in, w), (hid_in.at[0, pl.ds(0, 256)], hid.at[pl.ds(0, 256)]),
            (hid_in.at[0, pl.ds(256, 256)], hid.at[pl.ds(256, 256)]), (tgt_in, tgt), (area_in, area), (rid_in, rid),
        ])
    ]
    started(loads)
    barrier = pltpu.get_barrier_semaphore()
    peers = [mem_peer(d) for d in range(1, 8)] + [y_peer(d) for d in range(1, 4)]
    peers += [z_peer(1), z_peer(15)] + [near_peer(d) for d in NEAR]
    peers += [block_peer(0, dy, 1) for dy in (1, 2, 3)]
    for peer in peers:
        pl.semaphore_signal(barrier, inc=1, device_id=peer, device_id_type=LOGICAL)

    row, col = iota((128, VARS), 0), iota((128, VARS), 1)
    block, place = lax.shift_right_logical(row, 4), row & 15
    pick = jnp.where((col == block * VB + place) & (place < VB), 1.0, 0.0).astype(BF16)
    loads[0].wait()
    wp[...] = dot(pick, w[...], 1, 0).astype(BF16)
    for i in range(2):
        loads[1 + i].wait()
        cells = slice(256 * i, 256 * i + 256)
        pred = dot(wp[...], hid[cells], 1, 1).astype(BF16)
        psend[:, :, cells] = pred.reshape(MEMBERS, 16, 256)

    def tell(step):
        for side in (1, -1):
            peer = z_peer(16 + side * 2**step)
            pl.semaphore_signal(relay.at[step], inc=1, device_id=peer, device_id_type=LOGICAL)

    def hear(step):
        pl.semaphore_wait(relay.at[step], 2)

    pl.semaphore_wait(barrier, len(peers))
    started([
        copy(psend.at[mems[d]], precv.at[me], P1, P1, mem_peer(d))
        for d in MEM_STEPS
    ])
    tell(0)
    precv[pl.ds(me, 1)] = psend[pl.ds(me, 1)]

    for c in loads[3:]:
        c.wait()
    spot = jnp.where(place == 13, block, jnp.where((place == 14) & (block < VB - 8), block + 8, -1000))
    pick = jnp.where((spot >= 0) & (col == VB * me + spot), 1.0, 0.0).astype(BF16)
    tx[...] = dot(pick, tgt[...], 1, 0) + jnp.where(iota((128, 512), 0) == 15, 1.0, 0.0)

    ids = rid[...]
    mids, coarses = lax.shift_right_logical(ids, 4), lax.shift_right_logical(ids, 8)
    row = iota((8, 512), 0)
    key = jnp.where(row < 2, ids, jnp.where(row < 4, mids, coarses))
    ends = jnp.where(row % 2 == 0, key[:, 0:1], key[:, 511:512])
    label = jnp.where(row < 4, ends, row - 4)
    edge_high, edge_low = two_parts(jnp.where(key == label, area[...], 0.0))
    edge = jnp.concatenate([edge_high, edge_low], axis=0).astype(BF16)
    label_lane = jnp.where((iota((8, 128), 1) == 31) & (iota((8, 128), 0) < 4), label[:, 0:128].astype(F32), 0.0)

    turned = lambda a: jnp.transpose(jnp.broadcast_to(a, (128, 512)))
    ids_col = turned(ids.astype(F32))
    high_col, low_col = two_parts(turned(area[...]))
    for j in range(4):
        lanes = slice(128 * j, 128 * j + 128)
        same = ids_col == ids[:, lanes].astype(F32)
        sum_high[:, lanes] = jnp.where(same, high_col, 0.0).astype(BF16)
        sum_low[:, lanes] = jnp.where(same, low_col, 0.0).astype(BF16)
    first_id, last_id = ids[:, 0:1], ids[:, 511:512]
    first_mid, last_mid = mids[:, 0:1], mids[:, 511:512]
    same = lax.shift_right_logical(ids_col.astype(I32), 4) == iota((512, 128), 1) + first_mid
    mid_high[...] = jnp.where(same, high_col, 0.0).astype(BF16)
    mid_low[...] = jnp.where(same, low_col, 0.0).astype(BF16)
    inner = (mids == iota((128, 512), 0) + first_mid) & (mids != first_mid) & (mids != last_mid)
    spread[...] = jnp.where(inner, 1.0, 0.0).astype(BF16)

    hear(0)
    tell(1)
    arrived(precv.at[pl.ds(0, 7)], P1)
    values = (precv[...].reshape(128, 512).astype(F32) + tx[...]).astype(BF16)
    xs[...] = values
    pooled = dot(edge, values, 1, 1)
    msend[...] = pooled[0:8] + pooled[8:16] + label_lane
    started([
        copy(msend, nrecv.at[k], PN, PN, near_peer(d)) for k, d in enumerate(NEAR)
    ])

    hear(1)
    tell(2)
    kept = (iota((128, 128), 0) & 15) < VB
    fine[...] = dot(values, sum_high[...], 1, 0) + dot(values, sum_low[...], 1, 0)
    table = pooled_slopes(dot(values, mid_high[...], 1, 0) + dot(values, mid_low[...], 1, 0))
    table_high, table_low = two_parts(table)
    middle[...] = dot(table_high.astype(BF16), spread[...], 1, 0) + dot(table_low.astype(BF16), spread[...], 1, 0)

    def inner_slopes(j, carry):
        lanes = pl.ds(pl.multiple_of(j * 128, 128), 128)
        here = rid[:, lanes]
        alone = (here != first_id) & (here != last_id)
        slope = packed_slopes(xs[:, lanes].astype(F32)) + middle[:, lanes]
        total[:, lanes] = slope + jnp.where(alone, pooled_slopes(fine[:, lanes]), 0.0)
        return carry

    started([
        copy(msend, yrecv.at[d - 1], PY, PY, y_peer(d)) for d in range(1, 4)
    ])
    lax.fori_loop(0, 4, inner_slopes, 0)

    arrived(nrecv, PN)
    after_2, after, before, before_2 = [nrecv[k] for k in range(4)]
    edges = msend[...]

    def joined(at, others):
        line = edges[at : at + 1]
        for other in others:
            line = line + jnp.where(other[:, 31:32] == edges[at : at + 1, 31:32], other, 0.0)
        return line

    around = [before[3:4], before_2[3:4], after[2:3], after_2[2:3]]
    lines = [joined(0, [before[1:2]]), joined(1, [after[0:1]]), joined(2, around), joined(3, around)]
    ends = pooled_slopes(jnp.transpose(jnp.concatenate(lines + [jnp.zeros((124, 128), F32)], axis=0)))
    columns = [jnp.broadcast_to(ends[:, k : k + 1], (128, 128)) for k in range(4)]

    def all_slopes(j, carry):
        lanes = pl.ds(pl.multiple_of(j * 128, 128), 128)
        here = rid[:, lanes]
        mid = lax.shift_right_logical(here, 4)
        slope = total[:, lanes]
        slope = slope + jnp.where(here == first_id, columns[0], jnp.where(here == last_id, columns[1], 0.0))
        slope = slope + jnp.where(mid == first_mid, columns[2], jnp.where(mid == last_mid, columns[3], 0.0))
        part = jnp.where(kept, area[:, lanes] * slope, 0.0)
        gsend[:, :, lanes] = part.astype(BF16).reshape(MEMBERS, 16, 128)
        return carry

    lax.fori_loop(0, 4, all_slopes, 0)
    started([
        copy(gsend.at[mems[d]], grecv.at[me], P3, P3, mem_peer(d))
        for d in MEM_STEPS
    ])
    grecv[pl.ds(me, 1)] = gsend[pl.ds(me, 1)]

    hear(2)
    arrived(yrecv, PY)
    zsend[...] = (msend[...] + yrecv[0] + yrecv[1] + yrecv[2])[4:8]
    started([
        copy(zsend, zrecv.at[d - 1], PZ, PZ, z_peer(d)) for d in FAR_FIRST
    ])
    moment = dot(edge, hid[...], 1, 0)
    moment = (moment[0:8] + moment[8:16])[4:8]
    for j in range(8):
        at = 128 * ((j % 2) * 4 + j // 2)
        hsend[j] = moment[:, at : at + 128]
    started([
        copy(hsend.at[mems[d]], h1.at[me], H1, H1, mem_peer(d)) for d in MEM_STEPS
    ])
    h1[pl.ds(me, 1)] = hsend[pl.ds(me, 1)]
    arrived(grecv.at[pl.ds(0, 7)], P3)
    delta = grecv[...].reshape(128, 512)

    def weight_part(half, k):
        lanes = pl.ds(pl.multiple_of(half * 512 + 256 * k, 256), 256)
        product = dot(delta, hid[:, lanes], 1, 0)
        return [product[:, 128 * i : 128 * i + 128].reshape(8, 16, 128) for i in range(2)]

    cc = []
    for k in range(2):
        for i, part in enumerate(weight_part(1 - core, k)):
            csend[2 * k + i] = part.astype(BF16)
        cc += started([
            copy(csend.at[pl.ds(2 * k, 2)], crecv.at[pl.ds(2 * k, 2)], RC + k, RC + k, core_peer)
        ])
    for k in range(2):
        for i, part in enumerate(weight_part(core, k)):
            own[2 * k + i] = part
    arrived(zrecv, PZ)
    coarse_sum = zsend[...]
    for d in range(15):
        coarse_sum = coarse_sum + zrecv[d]
    coarse = jnp.transpose(jnp.concatenate([coarse_sum, jnp.zeros((124, 128), F32)], axis=0))
    inverse_area = ALL_CELLS / jnp.sum(coarse[15:16, 0:4], axis=1, keepdims=True)
    coarse_slope = jnp.where(kept, pooled_slopes(coarse), 0.0).reshape(MEMBERS, 16, 128)
    tile_send[...] = jnp.concatenate(
        [coarse_slope[m, :, 0:4] for m in range(MEMBERS)] + [jnp.zeros((16, 96), F32)], axis=1
    )
    coarse_send[...] = coarse_slope
    row_block = 2 * y + pair
    to_owner = [copy(tile_send, tile, CO, CO, mem_peer(d)) for d in MEM_STEPS]

    @pl.when(me == row_block)
    def _():
        started(to_owner)
        tile[...] = tile_send[...]

    def block_copy(i, dx, dy, dz):
        slot = dx * 8 + dy * 2 + dz
        peer = rows[dz][dy] + 2 * i
        return copy(bsend.at[i, 2 * ys_at[dy] + pairs[dz]], brecv.at[slot], RB, RB, peer)

    for k in range(2):
        cc[k].wait_recv()
        for i in (2 * k, 2 * k + 1):
            both = own[i] + crecv[i].astype(F32)
            own[i] = both
            bsend[i] = both.astype(BF16)
        for i in (2 * k, 2 * k + 1):
            dx = lax.rem(i - x + 4, 4)
            for dy, dz in NEARBY:
                block_copy(i, dx, dy, dz).start()

            @pl.when(dx != 0)
            def _():
                block_copy(i, dx, 0, 0).start()

    arrived(h1.at[pl.ds(0, 7)], H1)
    moments = jnp.concatenate([h1[m] for m in range(8)], axis=0)
    h2send[...] = moments.astype(BF16)
    started([
        copy(h2send, h2.at[i], H2, H2, block_peer(0, dy, dz)) for i, (dy, dz) in enumerate(NEARBY)
    ])
    arrived(h2, H2)
    for i in range(7):
        moments = moments + h2[i].astype(F32)

    @pl.when(me != row_block)
    def _():
        to_owner[0].wait_recv()

    piece = own[x, 2 * y + pair]
    share = tile[...]
    for i in range(32):
        piece = piece + share[:, i : i + 1] * moments[i : i + 1, :]
    arrived(brecv.at[pl.ds(1, 31)], RB)
    for dx, dy, dz in BLOCK:
        piece = piece + brecv[(dx * 4 + dy) * 2 + dz].astype(F32)
    piece = piece * inverse_area

    layer = lax.div(z, 2)
    strip[layer] = piece.astype(BF16)
    started([
        copy(
            strip.at[layer], strip.at[layer], SZ, SZ,
            z_peer(2 * d),
        )
        for d in (4, 3, 5, 2, 6, 1, 7)
    ])
    started([
        copy(coarse_send.at[mems[d]], coarse_mine.at[me], CM, CM, mem_peer(d))
        for d in MEM_STEPS
    ])
    coarse_mine[pl.ds(me, 1)] = coarse_send[pl.ds(me, 1)]
    sent(psend.at[pl.ds(0, 7)], P1)
    sent(nrecv, PN)
    sent(yrecv, PY)
    sent(gsend.at[pl.ds(0, 7)], P3)
    sent(zrecv, PZ)
    sent(h1.at[pl.ds(0, 7)], H1)
    sent(h2, H2)
    sent(brecv.at[pl.ds(1, 31)], RB)
    for c in cc:
        c.wait_send()

    @pl.when(me == row_block)
    def _():
        sent(coarse_send.at[pl.ds(0, 7)], CO)

    arrived(coarse_mine.at[pl.ds(0, 7)], CM)
    sent(coarse_send.at[pl.ds(0, 7)], CM)
    columns = [jnp.broadcast_to(coarse_mine[...].reshape(128, 128)[:, k : k + 1], (128, 128)) for k in range(4)]

    def gradient(j, carry):
        lanes = pl.ds(pl.multiple_of(j * 128, 128), 128)
        key = lax.shift_right_logical(rid[:, lanes], 8)
        slope = jnp.zeros((128, 128), F32)
        for k in range(4):
            slope = jnp.where(key == k, columns[k], slope)
        part = grecv[:, :, lanes].reshape(128, 128).astype(F32)
        grad[:, lanes] = ((part + area[:, lanes] * slope) * inverse_area).astype(BF16)
        return carry

    lax.fori_loop(0, 4, gradient, 0)
    arrived(strip.at[pl.ds(0, 7)], SZ)
    piece = strip[0].astype(F32)
    for k in range(1, 8):
        piece = piece + strip[k].astype(F32)
    chunk = core * 4 + x
    full[chunk, row_block] = piece.astype(BF16)

    spot = full.at[chunk, row_block]
    started([copy(spot, spot, GB, GB + at[0], block_peer(*at)) for i, at in enumerate(BLOCK)])
    gh[0] = dot(grad[...], wp[...], 0, 0).astype(BF16)
    sent(strip.at[pl.ds(0, 7)], SZ)
    for dx in (0, 1, 3, 2):
        arrived(full.at[0, pl.ds(0, 8 if dx else 7)], GB + dx)
        spot = full.at[core * 4 + xs_at[(4 - dx) % 4]]
        started([copy(spot, spot, GC, GC, core_peer)])
    sent(brecv.at[pl.ds(1, 31)], GB)
    arrived(full.at[pl.ds(0, 4)], GC)

    square = jnp.zeros((16, 128), F32)
    for k in range(8):
        part = full[k].astype(F32)
        square = square + jnp.sum(part * part, axis=0)
    mean_square = jnp.sum(square, keepdims=True) * (1.0 / (VARS * 1024))
    scale = lax.rsqrt(mean_square + 1e-06)
    for k in range(8):
        for j in range(8):
            rows = min(VB, VARS - VB * j)
            gw[VB * j : VB * j + rows, 128 * k : 128 * k + 128] = (full[k, j].astype(F32) * scale)[0:rows]

    sent(full.at[pl.ds(0, 4)], GC)


def write_out(gh, gw, gh_out, gw_out, done):
    copies = [pltpu.make_async_copy(gh, gh_out, done.at[0]), pltpu.make_async_copy(gw, gw_out, done.at[1])]
    for c in copies:
        c.start()
    for c in copies:
        c.wait()


def local(hidden_states, targets, cell_area, region_ids, decoder_weight):
    anywhere = pl.BlockSpec(memory_space=pl.ANY)
    vmem = pl.BlockSpec(memory_space=pltpu.VMEM)
    scratch = [
        ((512, 1024), BF16), ((VARS, 512), BF16), ((1, 512), F32), ((1, 512), I32), ((VARS, 1024), BF16),
        ((128, 1024), BF16), ((128, 512), F32), ((128, 512), BF16),
        ((8, 16, 512), BF16), ((8, 16, 512), BF16), ((8, 16, 512), BF16), ((8, 16, 512), BF16),
        ((512, 512), BF16), ((512, 512), BF16), ((512, 128), BF16), ((512, 128), BF16), ((128, 512), BF16),
        ((128, 512), F32), ((128, 512), F32), ((128, 512), F32),
        ((8, 128), F32), ((3, 8, 128), F32), ((4, 8, 128), F32), ((4, 128), F32), ((15, 4, 128), F32),
        ((4, 8, 16, 128), BF16), ((4, 8, 16, 128), BF16), ((4, 8, 16, 128), F32), ((4, 8, 16, 128), BF16),
        ((32, 16, 128), BF16), ((8, 16, 128), BF16), ((8, 8, 16, 128), BF16),
        ((8, 4, 128), F32), ((8, 4, 128), F32), ((32, 128), BF16), ((7, 32, 128), BF16),
        ((8, 16, 128), F32), ((8, 16, 128), F32), ((16, 128), F32), ((16, 128), F32), ((128, 512), BF16),
    ]
    arguments = (
        hidden_states, targets, cell_area.reshape(1, -1), region_ids.reshape(1, -1), decoder_weight.T
    )
    results = (
        jax.ShapeDtypeStruct(hidden_states.shape, BF16),
        jax.ShapeDtypeStruct((VARS, 1024), F32),
    )
    grad_hidden, grad_weight = pl.pallas_call(
        kernel,
        out_shape=results,
        in_specs=[anywhere] * 5,
        out_specs=(vmem, vmem),
        scratch_shapes=[pltpu.VMEM(s, t) for s, t in scratch]
        + [pltpu.SemaphoreType.DMA((n,)) for n in (6, COUNT, COUNT)]
        + [pltpu.SemaphoreType.REGULAR((3,))],
        compiler_params=pltpu.CompilerParams(
            collective_id=0, has_side_effects=True, vmem_limit_bytes=VMEM_LIMIT
        ),
    )(*[pltpu.with_memory_space_constraint(a, pltpu.HBM) for a in arguments])
    grad_hidden, grad_weight = pl.pallas_call(
        write_out,
        out_shape=results,
        in_specs=[vmem] * 2,
        out_specs=(anywhere, anywhere),
        scratch_shapes=[pltpu.SemaphoreType.DMA((2,))],
    )(*[pltpu.with_memory_space_constraint(a, pltpu.VMEM) for a in (grad_hidden, grad_weight)])
    return grad_hidden, grad_weight.T


def solution(mesh):
    in_specs = (P("mem", "cell", None), P(None, "cell"), P("cell"), P("cell"), P())
    out_specs = (P("mem", "cell", None), P())
    return jax.shard_map(local, mesh=mesh, in_specs=in_specs, out_specs=out_specs, check_vma=False)
```

```python
import functools

import jax
import jax.numpy as jnp
from jax import lax
from jax.experimental import pallas as pl
from jax.experimental.pallas import tpu as pltpu
from jax.sharding import PartitionSpec as P

MESH = pl.DeviceIdType.MESH
F32, BF16, I32 = jnp.float32, jnp.bfloat16, jnp.int32
SMOOTH = 0.1
MEMBERS = 8
VARS = 100
VB = 13
ALL_CELLS = 32768
VMEM_LIMIT = 32 * 1024 * 1024
NEAR = (-2, -1, 1, 2)
BLOCK = [(dx, dy, dz) for dx in (2, 1, 3, 0) for dy in (2, 1, 3, 0) for dz in (1, 0) if dx or dy or dz]
NEARBY = [(dy, dz) for dy in (2, 1, 3, 0) for dz in (1, 0) if dy or dz]
MEM_STEPS = (4, 3, 5, 2, 6, 1, 7)
FAR_FIRST = sorted(range(1, 16), key=lambda d: abs(d - 8))
P1, PY, PN, PZ, P3, RC, RB, SZ, GB, GC, H1, H2, CM, CO, COUNT = 0, 1, 2, 3, 4, 5, 7, 8, 9, 13, 14, 15, 16, 17, 18


def dot(a, b, left, right):
    return lax.dot_general(a, b, (((left,), (right,)), ((), ())), preferred_element_type=F32)


def iota(shape, axis):
    return lax.broadcasted_iota(I32, shape, axis)


def two_parts(a):
    high = a.astype(BF16).astype(F32)
    return high, (a - high).astype(BF16).astype(F32)


def slopes(members, target):
    ratio = lambda d: d * lax.rsqrt(d * d + SMOOTH * SMOOTH)
    pair = [None] * MEMBERS
    for m in range(MEMBERS):
        for n in range(m + 1, MEMBERS):
            term = ratio(members[m] - members[n])
            pair[m] = term if pair[m] is None else pair[m] + term
            pair[n] = -term if pair[n] is None else pair[n] - term
    return [
        ratio(members[m] - target) * (1.0 / MEMBERS) - pair[m] * (1.0 / (MEMBERS * (MEMBERS - 1)))
        for m in range(MEMBERS)
    ]


def packed_slopes(packed):
    width = packed.shape[1]
    members = [packed[m * 16 : m * 16 + 16] for m in range(MEMBERS)]
    row = iota((16, width), 0)
    target = jnp.zeros((16, width), F32)
    for v in range(VB):
        at = target_row(v)
        target = jnp.where(row == v, packed[at : at + 1], target)
    return jnp.concatenate(slopes(members, target), axis=0)


def target_row(v):
    return (v % 8) * 16 + 13 + v // 8


def pooled_slopes(packed):
    area = packed[15:16]
    return packed_slopes(packed * (1.0 / jnp.where(area > 0.0, area, 1.0)))


def kernel(
    hid_in, tgt_in, area_in, rid_in, w_in, gh, gw,
    hid, tgt, area, rid, w, wp, tx, xs, psend, precv, gsend, grecv, sum_high, sum_low, mid_high, mid_low, spread,
    fine, middle, total, msend, yrecv, nrecv, zsend, zrecv,
    csend, crecv, own, bsend, brecv, strip, full, hsend, h1, h2send, h2, coarse_send, coarse_mine, tile_send, tile, grad, load, send, recv, relay,
):
    me, ce = lax.axis_index("mem"), lax.axis_index("cell")
    x, core = lax.div(me, 2), lax.rem(me, 2)
    z, y = lax.div(ce, 4), lax.rem(ce, 4)
    mem_peer = lambda d: {"mem": lax.rem(me + d, 8)}
    core_peer = {"mem": me + 1 - 2 * core}
    pair = lax.rem(z, 2)
    block_peer = lambda dx, dy, dz: {
        "mem": lax.rem(x + dx, 4) * 2 + core, "cell": (z + dz * (1 - 2 * pair)) * 4 + lax.rem(y + dy, 4)
    }
    y_peer = lambda d: {"cell": z * 4 + lax.rem(y + d, 4)}
    z_peer = lambda d: {"cell": lax.rem(z + d, 16) * 4 + y}
    near_peer = lambda d: {"cell": lax.rem(ce + 64 + d, 64)}

    def copy(source, landing, s, r, peer):
        return pltpu.make_async_remote_copy(
            src_ref=source, dst_ref=landing, send_sem=send.at[s], recv_sem=recv.at[r],
            device_id=peer, device_id_type=MESH,
        )

    def arrived(array, group):
        copy(array, array, group, group, core_peer).wait_recv()

    def sent(array, group):
        copy(array, array, group, group, core_peer).wait_send()

    def started(copies):
        for c in copies:
            c.start()
        return copies

    loads = [
        pltpu.make_async_copy(source, landing, load.at[i])
        for i, (source, landing) in enumerate([
            (w_in, w), (hid_in.at[0, pl.ds(0, 256)], hid.at[pl.ds(0, 256)]),
            (hid_in.at[0, pl.ds(256, 256)], hid.at[pl.ds(256, 256)]), (tgt_in, tgt), (area_in, area), (rid_in, rid),
        ])
    ]
    started(loads)
    barrier = pltpu.get_barrier_semaphore()
    peers = [mem_peer(d) for d in range(1, 8)] + [y_peer(d) for d in range(1, 4)]
    peers += [z_peer(1), z_peer(15)] + [near_peer(d) for d in NEAR]
    peers += [block_peer(0, dy, 1) for dy in (1, 2, 3)]
    for peer in peers:
        pl.semaphore_signal(barrier, inc=1, device_id=peer, device_id_type=MESH)

    row, col = iota((128, VARS), 0), iota((128, VARS), 1)
    block, place = lax.shift_right_logical(row, 4), row & 15
    pick = jnp.where((col == block * VB + place) & (place < VB), 1.0, 0.0).astype(BF16)
    loads[0].wait()
    wp[...] = dot(pick, w[...], 1, 0).astype(BF16)
    for i in range(2):
        loads[1 + i].wait()
        cells = slice(256 * i, 256 * i + 256)
        pred = dot(wp[...], hid[cells], 1, 1).astype(BF16)
        psend[:, :, cells] = pred.reshape(MEMBERS, 16, 256)

    def tell(step):
        for side in (1, -1):
            peer = z_peer(16 + side * 2**step)
            pl.semaphore_signal(relay.at[step], inc=1, device_id=peer, device_id_type=MESH)

    def hear(step):
        pl.semaphore_wait(relay.at[step], 2)

    pl.semaphore_wait(barrier, len(peers))
    started([
        copy(psend.at[lax.rem(me + d, 8)], precv.at[me], P1, P1, mem_peer(d))
        for d in MEM_STEPS
    ])
    tell(0)
    precv[pl.ds(me, 1)] = psend[pl.ds(me, 1)]

    for c in loads[3:]:
        c.wait()
    spot = jnp.where(place == 13, block, jnp.where((place == 14) & (block < VB - 8), block + 8, -1000))
    pick = jnp.where((spot >= 0) & (col == VB * me + spot), 1.0, 0.0).astype(BF16)
    tx[...] = dot(pick, tgt[...], 1, 0) + jnp.where(iota((128, 512), 0) == 15, 1.0, 0.0)

    ids = rid[...]
    mids, coarses = lax.shift_right_logical(ids, 4), lax.shift_right_logical(ids, 8)
    row = iota((8, 512), 0)
    key = jnp.where(row < 2, ids, jnp.where(row < 4, mids, coarses))
    ends = jnp.where(row % 2 == 0, key[:, 0:1], key[:, 511:512])
    label = jnp.where(row < 4, ends, row - 4)
    edge_high, edge_low = two_parts(jnp.where(key == label, area[...], 0.0))
    edge = jnp.concatenate([edge_high, edge_low], axis=0).astype(BF16)
    label_lane = jnp.where((iota((8, 128), 1) == 31) & (iota((8, 128), 0) < 4), label[:, 0:128].astype(F32), 0.0)

    turned = lambda a: jnp.transpose(jnp.broadcast_to(a, (128, 512)))
    ids_col = turned(ids.astype(F32))
    high_col, low_col = two_parts(turned(area[...]))
    for j in range(4):
        lanes = slice(128 * j, 128 * j + 128)
        same = ids_col == ids[:, lanes].astype(F32)
        sum_high[:, lanes] = jnp.where(same, high_col, 0.0).astype(BF16)
        sum_low[:, lanes] = jnp.where(same, low_col, 0.0).astype(BF16)
    first_id, last_id = ids[:, 0:1], ids[:, 511:512]
    first_mid, last_mid = mids[:, 0:1], mids[:, 511:512]
    same = lax.shift_right_logical(ids_col.astype(I32), 4) == iota((512, 128), 1) + first_mid
    mid_high[...] = jnp.where(same, high_col, 0.0).astype(BF16)
    mid_low[...] = jnp.where(same, low_col, 0.0).astype(BF16)
    inner = (mids == iota((128, 512), 0) + first_mid) & (mids != first_mid) & (mids != last_mid)
    spread[...] = jnp.where(inner, 1.0, 0.0).astype(BF16)

    hear(0)
    tell(1)
    arrived(precv.at[pl.ds(0, 7)], P1)
    values = (precv[...].reshape(128, 512).astype(F32) + tx[...]).astype(BF16)
    xs[...] = values
    pooled = dot(edge, values, 1, 1)
    msend[...] = pooled[0:8] + pooled[8:16] + label_lane
    started([
        copy(msend, nrecv.at[k], PN, PN, near_peer(d)) for k, d in enumerate(NEAR)
    ])

    started([
        copy(msend, yrecv.at[d - 1], PY, PY, y_peer(d)) for d in range(1, 4)
    ])
    hear(1)
    tell(2)
    kept = (iota((128, 128), 0) & 15) < VB
    fine[...] = dot(values, sum_high[...], 1, 0) + dot(values, sum_low[...], 1, 0)
    table = pooled_slopes(dot(values, mid_high[...], 1, 0) + dot(values, mid_low[...], 1, 0))
    table_high, table_low = two_parts(table)
    middle[...] = dot(table_high.astype(BF16), spread[...], 1, 0) + dot(table_low.astype(BF16), spread[...], 1, 0)

    def inner_slopes(j, carry):
        lanes = pl.ds(pl.multiple_of(j * 128, 128), 128)
        here = rid[:, lanes]
        alone = (here != first_id) & (here != last_id)
        slope = packed_slopes(xs[:, lanes].astype(F32)) + middle[:, lanes]
        total[:, lanes] = slope + jnp.where(alone, pooled_slopes(fine[:, lanes]), 0.0)
        return carry

    lax.fori_loop(0, 4, inner_slopes, 0)

    arrived(nrecv, PN)
    after_2, after, before, before_2 = [nrecv[k] for k in range(4)]
    edges = msend[...]

    def joined(at, others):
        line = edges[at : at + 1]
        for other in others:
            line = line + jnp.where(other[:, 31:32] == edges[at : at + 1, 31:32], other, 0.0)
        return line

    around = [before[3:4], before_2[3:4], after[2:3], after_2[2:3]]
    lines = [joined(0, [before[1:2]]), joined(1, [after[0:1]]), joined(2, around), joined(3, around)]
    ends = pooled_slopes(jnp.transpose(jnp.concatenate(lines + [jnp.zeros((124, 128), F32)], axis=0)))
    columns = [jnp.broadcast_to(ends[:, k : k + 1], (128, 128)) for k in range(4)]

    def all_slopes(j, carry):
        lanes = pl.ds(pl.multiple_of(j * 128, 128), 128)
        here = rid[:, lanes]
        mid = lax.shift_right_logical(here, 4)
        slope = total[:, lanes]
        slope = slope + jnp.where(here == first_id, columns[0], jnp.where(here == last_id, columns[1], 0.0))
        slope = slope + jnp.where(mid == first_mid, columns[2], jnp.where(mid == last_mid, columns[3], 0.0))
        part = jnp.where(kept, area[:, lanes] * slope, 0.0)
        gsend[:, :, lanes] = part.astype(BF16).reshape(MEMBERS, 16, 128)
        return carry

    lax.fori_loop(0, 4, all_slopes, 0)
    started([
        copy(gsend.at[lax.rem(me + d, 8)], grecv.at[me], P3, P3, mem_peer(d))
        for d in MEM_STEPS
    ])
    grecv[pl.ds(me, 1)] = gsend[pl.ds(me, 1)]

    hear(2)
    arrived(yrecv, PY)
    zsend[...] = (msend[...] + yrecv[0] + yrecv[1] + yrecv[2])[4:8]
    started([
        copy(zsend, zrecv.at[d - 1], PZ, PZ, z_peer(d)) for d in FAR_FIRST
    ])
    moment = dot(edge, hid[...], 1, 0)
    moment = (moment[0:8] + moment[8:16])[4:8]
    for j in range(8):
        at = 128 * ((j % 2) * 4 + j // 2)
        hsend[j] = moment[:, at : at + 128]
    started([
        copy(hsend.at[lax.rem(me + d, 8)], h1.at[me], H1, H1, mem_peer(d)) for d in MEM_STEPS
    ])
    h1[pl.ds(me, 1)] = hsend[pl.ds(me, 1)]
    arrived(grecv.at[pl.ds(0, 7)], P3)
    delta = grecv[...].reshape(128, 512)

    def weight_part(half, k):
        lanes = pl.ds(pl.multiple_of(half * 512 + 256 * k, 256), 256)
        product = dot(delta, hid[:, lanes], 1, 0)
        return [product[:, 128 * i : 128 * i + 128].reshape(8, 16, 128) for i in range(2)]

    cc = []
    for k in range(2):
        for i, part in enumerate(weight_part(1 - core, k)):
            csend[2 * k + i] = part.astype(BF16)
        cc += started([
            copy(csend.at[pl.ds(2 * k, 2)], crecv.at[pl.ds(2 * k, 2)], RC + k, RC + k, core_peer)
        ])
    for k in range(2):
        for i, part in enumerate(weight_part(core, k)):
            own[2 * k + i] = part
    arrived(h1.at[pl.ds(0, 7)], H1)
    moments = jnp.concatenate([h1[m] for m in range(8)], axis=0)
    h2send[...] = moments.astype(BF16)
    started([
        copy(h2send, h2.at[i], H2, H2, block_peer(0, dy, dz)) for i, (dy, dz) in enumerate(NEARBY)
    ])

    def block_copy(dx, dy, dz):
        slot = (dx * 4 + dy) * 2 + dz
        to = lax.rem(x + dx, 4), 2 * lax.rem(y + dy, 4) + pair + dz * (1 - 2 * pair)
        return copy(bsend.at[to], brecv.at[slot], RB, RB, block_peer(dx, dy, dz))

    for k in range(2):
        cc[k].wait_recv()
        for i in (2 * k, 2 * k + 1):
            both = own[i] + crecv[i].astype(F32)
            own[i] = both
            bsend[i] = both.astype(BF16)
        for i in (2 * k, 2 * k + 1):
            dx = lax.rem(i - x + 4, 4)
            for dy, dz in NEARBY:
                block_copy(dx, dy, dz).start()

            @pl.when(dx != 0)
            def _():
                block_copy(dx, 0, 0).start()

    arrived(zrecv, PZ)
    coarse_sum = zsend[...]
    for d in range(15):
        coarse_sum = coarse_sum + zrecv[d]
    coarse = jnp.transpose(jnp.concatenate([coarse_sum, jnp.zeros((124, 128), F32)], axis=0))
    inverse_area = ALL_CELLS / jnp.sum(coarse[15:16, 0:4], axis=1, keepdims=True)
    coarse_slope = jnp.where(kept, pooled_slopes(coarse), 0.0).reshape(MEMBERS, 16, 128)
    tile_send[...] = jnp.concatenate(
        [coarse_slope[m, :, 0:4] for m in range(MEMBERS)] + [jnp.zeros((16, 96), F32)], axis=1
    )
    coarse_send[...] = coarse_slope
    row_block = 2 * y + pair
    to_owner = [copy(tile_send, tile, CO, CO, mem_peer(d)) for d in MEM_STEPS]

    @pl.when(me == row_block)
    def _():
        started(to_owner)
        tile[...] = tile_send[...]

    arrived(h2, H2)
    for i in range(7):
        moments = moments + h2[i].astype(F32)

    @pl.when(me != row_block)
    def _():
        to_owner[0].wait_recv()

    piece = own[x, 2 * y + pair]
    share = tile[...]
    for i in range(32):
        piece = piece + share[:, i : i + 1] * moments[i : i + 1, :]
    arrived(brecv.at[pl.ds(1, 31)], RB)
    for dx, dy, dz in BLOCK:
        piece = piece + brecv[(dx * 4 + dy) * 2 + dz].astype(F32)
    piece = piece * inverse_area

    layer = lax.div(z, 2)
    strip[layer] = piece.astype(BF16)
    started([
        copy(
            strip.at[layer], strip.at[layer], SZ, SZ,
            {"cell": (lax.rem(layer + d, 8) * 2 + pair) * 4 + y},
        )
        for d in (4, 3, 5, 2, 6, 1, 7)
    ])
    started([
        copy(coarse_send.at[lax.rem(me + d, 8)], coarse_mine.at[me], CM, CM, mem_peer(d))
        for d in MEM_STEPS
    ])
    coarse_mine[pl.ds(me, 1)] = coarse_send[pl.ds(me, 1)]
    sent(psend.at[pl.ds(0, 7)], P1)
    sent(nrecv, PN)
    sent(yrecv, PY)
    sent(gsend.at[pl.ds(0, 7)], P3)
    sent(zrecv, PZ)
    sent(h1.at[pl.ds(0, 7)], H1)
    sent(h2, H2)
    sent(brecv.at[pl.ds(1, 31)], RB)
    for c in cc:
        c.wait_send()

    @pl.when(me == row_block)
    def _():
        sent(coarse_send.at[pl.ds(0, 7)], CO)

    arrived(coarse_mine.at[pl.ds(0, 7)], CM)
    sent(coarse_send.at[pl.ds(0, 7)], CM)
    columns = [jnp.broadcast_to(coarse_mine[...].reshape(128, 128)[:, k : k + 1], (128, 128)) for k in range(4)]

    def gradient(j, carry):
        lanes = pl.ds(pl.multiple_of(j * 128, 128), 128)
        key = lax.shift_right_logical(rid[:, lanes], 8)
        slope = jnp.zeros((128, 128), F32)
        for k in range(4):
            slope = jnp.where(key == k, columns[k], slope)
        part = grecv[:, :, lanes].reshape(128, 128).astype(F32)
        grad[:, lanes] = ((part + area[:, lanes] * slope) * inverse_area).astype(BF16)
        return carry

    lax.fori_loop(0, 4, gradient, 0)
    arrived(strip.at[pl.ds(0, 7)], SZ)
    piece = strip[0].astype(F32)
    for k in range(1, 8):
        piece = piece + strip[k].astype(F32)
    chunk = core * 4 + x
    full[chunk, row_block] = piece.astype(BF16)

    spot = full.at[chunk, row_block]
    started([copy(spot, spot, GB, GB + at[0], block_peer(*at)) for i, at in enumerate(BLOCK)])
    gh[0] = dot(grad[...], wp[...], 0, 0).astype(BF16)
    sent(strip.at[pl.ds(0, 7)], SZ)
    for dx in (2, 1, 3, 0):
        arrived(full.at[0, pl.ds(0, 8 if dx else 7)], GB + dx)
        spot = full.at[core * 4 + lax.rem(x - dx + 4, 4)]
        started([copy(spot, spot, GC, GC, core_peer)])
    sent(brecv.at[pl.ds(1, 31)], GB)
    arrived(full.at[pl.ds(0, 4)], GC)

    square = jnp.zeros((16, 128), F32)
    for k in range(8):
        part = full[k].astype(F32)
        square = square + jnp.sum(part * part, axis=0)
    mean_square = jnp.sum(square, keepdims=True) * (1.0 / (VARS * 1024))
    scale = lax.rsqrt(mean_square + 1e-06)
    for k in range(8):
        for j in range(8):
            rows = min(VB, VARS - VB * j)
            gw[VB * j : VB * j + rows, 128 * k : 128 * k + 128] = (full[k, j].astype(F32) * scale)[0:rows]

    sent(full.at[pl.ds(0, 4)], GC)


def write_out(gh, gw, gh_out, gw_out, done):
    copies = [pltpu.make_async_copy(gh, gh_out, done.at[0]), pltpu.make_async_copy(gw, gw_out, done.at[1])]
    for c in copies:
        c.start()
    for c in copies:
        c.wait()


def local(hidden_states, targets, cell_area, region_ids, decoder_weight):
    anywhere = pl.BlockSpec(memory_space=pl.ANY)
    vmem = pl.BlockSpec(memory_space=pltpu.VMEM)
    scratch = [
        ((512, 1024), BF16), ((VARS, 512), BF16), ((1, 512), F32), ((1, 512), I32), ((VARS, 1024), BF16),
        ((128, 1024), BF16), ((128, 512), F32), ((128, 512), BF16),
        ((8, 16, 512), BF16), ((8, 16, 512), BF16), ((8, 16, 512), BF16), ((8, 16, 512), BF16),
        ((512, 512), BF16), ((512, 512), BF16), ((512, 128), BF16), ((512, 128), BF16), ((128, 512), BF16),
        ((128, 512), F32), ((128, 512), F32), ((128, 512), F32),
        ((8, 128), F32), ((3, 8, 128), F32), ((4, 8, 128), F32), ((4, 128), F32), ((15, 4, 128), F32),
        ((4, 8, 16, 128), BF16), ((4, 8, 16, 128), BF16), ((4, 8, 16, 128), F32), ((4, 8, 16, 128), BF16),
        ((32, 16, 128), BF16), ((8, 16, 128), BF16), ((8, 8, 16, 128), BF16),
        ((8, 4, 128), F32), ((8, 4, 128), F32), ((32, 128), BF16), ((7, 32, 128), BF16),
        ((8, 16, 128), F32), ((8, 16, 128), F32), ((16, 128), F32), ((16, 128), F32), ((128, 512), BF16),
    ]
    arguments = (
        hidden_states, targets, cell_area.reshape(1, -1), region_ids.reshape(1, -1), decoder_weight.T
    )
    results = (
        jax.ShapeDtypeStruct(hidden_states.shape, BF16),
        jax.ShapeDtypeStruct((VARS, 1024), F32),
    )
    grad_hidden, grad_weight = pl.pallas_call(
        kernel,
        out_shape=results,
        in_specs=[anywhere] * 5,
        out_specs=(vmem, vmem),
        scratch_shapes=[pltpu.VMEM(s, t) for s, t in scratch]
        + [pltpu.SemaphoreType.DMA((n,)) for n in (6, COUNT, COUNT)]
        + [pltpu.SemaphoreType.REGULAR((3,))],
        compiler_params=pltpu.CompilerParams(
            collective_id=0, has_side_effects=True, vmem_limit_bytes=VMEM_LIMIT
        ),
    )(*[pltpu.with_memory_space_constraint(a, pltpu.HBM) for a in arguments])
    grad_hidden, grad_weight = pl.pallas_call(
        write_out,
        out_shape=results,
        in_specs=[vmem] * 2,
        out_specs=(anywhere, anywhere),
        scratch_shapes=[pltpu.SemaphoreType.DMA((2,))],
    )(*[pltpu.with_memory_space_constraint(a, pltpu.VMEM) for a in (grad_hidden, grad_weight)])
    return grad_hidden, grad_weight.T


def solution(mesh):
    in_specs = (P("mem", "cell", None), P(None, "cell"), P("cell"), P("cell"), P())
    out_specs = (P("mem", "cell", None), P())
    return jax.shard_map(local, mesh=mesh, in_specs=in_specs, out_specs=out_specs, check_vma=False)
```

```python
import functools

import jax
import jax.numpy as jnp
from jax import lax
from jax.experimental import pallas as pl
from jax.experimental.pallas import tpu as pltpu
from jax.sharding import PartitionSpec as P

MESH = pl.DeviceIdType.MESH
F32, BF16, I32 = jnp.float32, jnp.bfloat16, jnp.int32
SMOOTH = 0.1
MEMBERS = 8
VARS = 100
VB = 13
ALL_CELLS = 32768
VMEM_LIMIT = 32 * 1024 * 1024
NEAR = (-2, -1, 1, 2)
BLOCK = [(dx, dy, dz) for dx in (2, 1, 3, 0) for dy in (2, 1, 3, 0) for dz in (1, 0) if dx or dy or dz]
NEARBY = [(dy, dz) for dy in (2, 1, 3, 0) for dz in (1, 0) if dy or dz]
MEM_STEPS = (4, 3, 5, 2, 6, 1, 7)
FAR_FIRST = sorted(range(1, 16), key=lambda d: abs(d - 8))
P1, PY, PN, PZ, P3, RC, RB, SZ, GB, GC, H1, H2, CM, CO, COUNT = 0, 1, 2, 3, 4, 5, 7, 8, 9, 13, 14, 15, 16, 17, 18


def dot(a, b, left, right):
    return lax.dot_general(a, b, (((left,), (right,)), ((), ())), preferred_element_type=F32)


def iota(shape, axis):
    return lax.broadcasted_iota(I32, shape, axis)


def two_parts(a):
    high = a.astype(BF16).astype(F32)
    return high, (a - high).astype(BF16).astype(F32)


def slopes(members, target):
    ratio = lambda d: d * lax.rsqrt(d * d + SMOOTH * SMOOTH)
    pair = [None] * MEMBERS
    for m in range(MEMBERS):
        for n in range(m + 1, MEMBERS):
            term = ratio(members[m] - members[n])
            pair[m] = term if pair[m] is None else pair[m] + term
            pair[n] = -term if pair[n] is None else pair[n] - term
    return [
        ratio(members[m] - target) * (1.0 / MEMBERS) - pair[m] * (1.0 / (MEMBERS * (MEMBERS - 1)))
        for m in range(MEMBERS)
    ]


def packed_slopes(packed):
    width = packed.shape[1]
    members = [packed[m * 16 : m * 16 + 16] for m in range(MEMBERS)]
    row = iota((16, width), 0)
    target = jnp.zeros((16, width), F32)
    for v in range(VB):
        at = target_row(v)
        target = jnp.where(row == v, packed[at : at + 1], target)
    return jnp.concatenate(slopes(members, target), axis=0)


def target_row(v):
    return (v % 8) * 16 + 13 + v // 8


def pooled_slopes(packed):
    area = packed[15:16]
    return packed_slopes(packed * (1.0 / jnp.where(area > 0.0, area, 1.0)))


def kernel(
    hid_in, tgt_in, area_in, rid_in, w_in, gh, gw,
    hid, tgt, area, rid, w, wp, tx, xs, psend, precv, gsend, grecv, sum_high, sum_low, mid_high, mid_low, spread,
    fine, middle, total, msend, yrecv, nrecv, zsend, zrecv,
    csend, crecv, own, bsend, brecv, strip, full, hsend, h1, h2send, h2, coarse_send, coarse_mine, tile_send, tile, grad, load, send, recv, relay,
):
    me, ce = lax.axis_index("mem"), lax.axis_index("cell")
    x, core = lax.div(me, 2), lax.rem(me, 2)
    z, y = lax.div(ce, 4), lax.rem(ce, 4)
    mem_peer = lambda d: {"mem": lax.rem(me + d, 8)}
    core_peer = {"mem": me + 1 - 2 * core}
    pair = lax.rem(z, 2)
    block_peer = lambda dx, dy, dz: {
        "mem": lax.rem(x + dx, 4) * 2 + core, "cell": (z + dz * (1 - 2 * pair)) * 4 + lax.rem(y + dy, 4)
    }
    y_peer = lambda d: {"cell": z * 4 + lax.rem(y + d, 4)}
    z_peer = lambda d: {"cell": lax.rem(z + d, 16) * 4 + y}
    near_peer = lambda d: {"cell": lax.rem(ce + 64 + d, 64)}

    def copy(source, landing, s, r, peer):
        return pltpu.make_async_remote_copy(
            src_ref=source, dst_ref=landing, send_sem=send.at[s], recv_sem=recv.at[r],
            device_id=peer, device_id_type=MESH,
        )

    def arrived(array, group):
        copy(array, array, group, group, core_peer).wait_recv()

    def sent(array, group):
        copy(array, array, group, group, core_peer).wait_send()

    def started(copies):
        for c in copies:
            c.start()
        return copies

    loads = [
        pltpu.make_async_copy(source, landing, load.at[i])
        for i, (source, landing) in enumerate([
            (w_in, w), (hid_in.at[0, pl.ds(0, 256)], hid.at[pl.ds(0, 256)]),
            (hid_in.at[0, pl.ds(256, 256)], hid.at[pl.ds(256, 256)]), (tgt_in, tgt), (area_in, area), (rid_in, rid),
        ])
    ]
    started(loads)
    barrier = pltpu.get_barrier_semaphore()
    peers = [mem_peer(d) for d in range(1, 8)] + [y_peer(d) for d in range(1, 4)]
    peers += [z_peer(1), z_peer(15)] + [near_peer(d) for d in NEAR]
    peers += [block_peer(0, dy, 1) for dy in (1, 2, 3)]
    for peer in peers:
        pl.semaphore_signal(barrier, inc=1, device_id=peer, device_id_type=MESH)

    row, col = iota((128, VARS), 0), iota((128, VARS), 1)
    block, place = lax.shift_right_logical(row, 4), row & 15
    pick = jnp.where((col == block * VB + place) & (place < VB), 1.0, 0.0).astype(BF16)
    loads[0].wait()
    wp[...] = dot(pick, w[...], 1, 0).astype(BF16)
    for i in range(2):
        loads[1 + i].wait()
        cells = slice(256 * i, 256 * i + 256)
        pred = dot(wp[...], hid[cells], 1, 1).astype(BF16)
        psend[:, :, cells] = pred.reshape(MEMBERS, 16, 256)

    def tell(step):
        for side in (1, -1):
            peer = z_peer(16 + side * 2**step)
            pl.semaphore_signal(relay.at[step], inc=1, device_id=peer, device_id_type=MESH)

    def hear(step):
        pl.semaphore_wait(relay.at[step], 2)

    pl.semaphore_wait(barrier, len(peers))
    started([
        copy(psend.at[lax.rem(me + d, 8)], precv.at[me], P1, P1, mem_peer(d))
        for d in MEM_STEPS
    ])
    tell(0)
    precv[pl.ds(me, 1)] = psend[pl.ds(me, 1)]

    for c in loads[3:]:
        c.wait()
    spot = jnp.where(place == 13, block, jnp.where((place == 14) & (block < VB - 8), block + 8, -1000))
    pick = jnp.where((spot >= 0) & (col == VB * me + spot), 1.0, 0.0).astype(BF16)
    tx[...] = dot(pick, tgt[...], 1, 0) + jnp.where(iota((128, 512), 0) == 15, 1.0, 0.0)

    ids = rid[...]
    mids, coarses = lax.shift_right_logical(ids, 4), lax.shift_right_logical(ids, 8)
    row = iota((8, 512), 0)
    key = jnp.where(row < 2, ids, jnp.where(row < 4, mids, coarses))
    ends = jnp.where(row % 2 == 0, key[:, 0:1], key[:, 511:512])
    label = jnp.where(row < 4, ends, row - 4)
    edge_high, edge_low = two_parts(jnp.where(key == label, area[...], 0.0))
    edge = jnp.concatenate([edge_high, edge_low], axis=0).astype(BF16)
    label_lane = jnp.where((iota((8, 128), 1) == 31) & (iota((8, 128), 0) < 4), label[:, 0:128].astype(F32), 0.0)

    turned = lambda a: jnp.transpose(jnp.broadcast_to(a, (128, 512)))
    ids_col = turned(ids.astype(F32))
    high_col, low_col = two_parts(turned(area[...]))
    for j in range(4):
        lanes = slice(128 * j, 128 * j + 128)
        same = ids_col == ids[:, lanes].astype(F32)
        sum_high[:, lanes] = jnp.where(same, high_col, 0.0).astype(BF16)
        sum_low[:, lanes] = jnp.where(same, low_col, 0.0).astype(BF16)
    first_id, last_id = ids[:, 0:1], ids[:, 511:512]
    first_mid, last_mid = mids[:, 0:1], mids[:, 511:512]
    same = lax.shift_right_logical(ids_col.astype(I32), 4) == iota((512, 128), 1) + first_mid
    mid_high[...] = jnp.where(same, high_col, 0.0).astype(BF16)
    mid_low[...] = jnp.where(same, low_col, 0.0).astype(BF16)
    inner = (mids == iota((128, 512), 0) + first_mid) & (mids != first_mid) & (mids != last_mid)
    spread[...] = jnp.where(inner, 1.0, 0.0).astype(BF16)

    hear(0)
    tell(1)
    arrived(precv.at[pl.ds(0, 7)], P1)
    values = (precv[...].reshape(128, 512).astype(F32) + tx[...]).astype(BF16)
    xs[...] = values
    pooled = dot(edge, values, 1, 1)
    msend[...] = pooled[0:8] + pooled[8:16] + label_lane
    started([
        copy(msend, nrecv.at[k], PN, PN, near_peer(d)) for k, d in enumerate(NEAR)
    ])

    hear(1)
    tell(2)
    kept = (iota((128, 128), 0) & 15) < VB
    fine[...] = dot(values, sum_high[...], 1, 0) + dot(values, sum_low[...], 1, 0)
    table = pooled_slopes(dot(values, mid_high[...], 1, 0) + dot(values, mid_low[...], 1, 0))
    table_high, table_low = two_parts(table)
    middle[...] = dot(table_high.astype(BF16), spread[...], 1, 0) + dot(table_low.astype(BF16), spread[...], 1, 0)

    def inner_slopes(j, carry):
        lanes = pl.ds(pl.multiple_of(j * 128, 128), 128)
        here = rid[:, lanes]
        alone = (here != first_id) & (here != last_id)
        slope = packed_slopes(xs[:, lanes].astype(F32)) + middle[:, lanes]
        total[:, lanes] = slope + jnp.where(alone, pooled_slopes(fine[:, lanes]), 0.0)
        return carry

    lax.fori_loop(0, 4, inner_slopes, 0)
    started([
        copy(msend, yrecv.at[d - 1], PY, PY, y_peer(d)) for d in range(1, 4)
    ])

    arrived(nrecv, PN)
    after_2, after, before, before_2 = [nrecv[k] for k in range(4)]
    edges = msend[...]

    def joined(at, others):
        line = edges[at : at + 1]
        for other in others:
            line = line + jnp.where(other[:, 31:32] == edges[at : at + 1, 31:32], other, 0.0)
        return line

    around = [before[3:4], before_2[3:4], after[2:3], after_2[2:3]]
    lines = [joined(0, [before[1:2]]), joined(1, [after[0:1]]), joined(2, around), joined(3, around)]
    ends = pooled_slopes(jnp.transpose(jnp.concatenate(lines + [jnp.zeros((124, 128), F32)], axis=0)))
    columns = [jnp.broadcast_to(ends[:, k : k + 1], (128, 128)) for k in range(4)]

    def all_slopes(j, carry):
        lanes = pl.ds(pl.multiple_of(j * 128, 128), 128)
        here = rid[:, lanes]
        mid = lax.shift_right_logical(here, 4)
        slope = total[:, lanes]
        slope = slope + jnp.where(here == first_id, columns[0], jnp.where(here == last_id, columns[1], 0.0))
        slope = slope + jnp.where(mid == first_mid, columns[2], jnp.where(mid == last_mid, columns[3], 0.0))
        part = jnp.where(kept, area[:, lanes] * slope, 0.0)
        gsend[:, :, lanes] = part.astype(BF16).reshape(MEMBERS, 16, 128)
        return carry

    lax.fori_loop(0, 4, all_slopes, 0)
    started([
        copy(gsend.at[lax.rem(me + d, 8)], grecv.at[me], P3, P3, mem_peer(d))
        for d in MEM_STEPS
    ])
    grecv[pl.ds(me, 1)] = gsend[pl.ds(me, 1)]

    hear(2)
    arrived(yrecv, PY)
    zsend[...] = (msend[...] + yrecv[0] + yrecv[1] + yrecv[2])[4:8]
    started([
        copy(zsend, zrecv.at[d - 1], PZ, PZ, z_peer(d)) for d in FAR_FIRST
    ])
    moment = dot(edge, hid[...], 1, 0)
    moment = (moment[0:8] + moment[8:16])[4:8]
    for j in range(8):
        at = 128 * ((j % 2) * 4 + j // 2)
        hsend[j] = moment[:, at : at + 128]
    started([
        copy(hsend.at[lax.rem(me + d, 8)], h1.at[me], H1, H1, mem_peer(d)) for d in MEM_STEPS
    ])
    h1[pl.ds(me, 1)] = hsend[pl.ds(me, 1)]
    arrived(grecv.at[pl.ds(0, 7)], P3)
    delta = grecv[...].reshape(128, 512)

    def weight_part(half, k):
        lanes = pl.ds(pl.multiple_of(half * 512 + 256 * k, 256), 256)
        product = dot(delta, hid[:, lanes], 1, 0)
        return [product[:, 128 * i : 128 * i + 128].reshape(8, 16, 128) for i in range(2)]

    cc = []
    for k in range(2):
        for i, part in enumerate(weight_part(1 - core, k)):
            csend[2 * k + i] = part.astype(BF16)
        cc += started([
            copy(csend.at[pl.ds(2 * k, 2)], crecv.at[pl.ds(2 * k, 2)], RC + k, RC + k, core_peer)
        ])
    for k in range(2):
        for i, part in enumerate(weight_part(core, k)):
            own[2 * k + i] = part
    def block_copy(dx, dy, dz):
        slot = (dx * 4 + dy) * 2 + dz
        to = lax.rem(x + dx, 4), 2 * lax.rem(y + dy, 4) + pair + dz * (1 - 2 * pair)
        return copy(bsend.at[to], brecv.at[slot], RB, RB, block_peer(dx, dy, dz))

    for k in range(2):
        cc[k].wait_recv()
        for i in (2 * k, 2 * k + 1):
            both = own[i] + crecv[i].astype(F32)
            own[i] = both
            bsend[i] = both.astype(BF16)
        for i in (2 * k, 2 * k + 1):
            dx = lax.rem(i - x + 4, 4)
            for dy, dz in NEARBY:
                block_copy(dx, dy, dz).start()

            @pl.when(dx != 0)
            def _():
                block_copy(dx, 0, 0).start()

    arrived(h1.at[pl.ds(0, 7)], H1)
    moments = jnp.concatenate([h1[m] for m in range(8)], axis=0)
    h2send[...] = moments.astype(BF16)
    started([
        copy(h2send, h2.at[i], H2, H2, block_peer(0, dy, dz)) for i, (dy, dz) in enumerate(NEARBY)
    ])
    arrived(zrecv, PZ)
    coarse_sum = zsend[...]
    for d in range(15):
        coarse_sum = coarse_sum + zrecv[d]
    coarse = jnp.transpose(jnp.concatenate([coarse_sum, jnp.zeros((124, 128), F32)], axis=0))
    inverse_area = ALL_CELLS / jnp.sum(coarse[15:16, 0:4], axis=1, keepdims=True)
    coarse_slope = jnp.where(kept, pooled_slopes(coarse), 0.0).reshape(MEMBERS, 16, 128)
    tile_send[...] = jnp.concatenate(
        [coarse_slope[m, :, 0:4] for m in range(MEMBERS)] + [jnp.zeros((16, 96), F32)], axis=1
    )
    coarse_send[...] = coarse_slope
    row_block = 2 * y + pair
    to_owner = [copy(tile_send, tile, CO, CO, mem_peer(d)) for d in MEM_STEPS]

    @pl.when(me == row_block)
    def _():
        started(to_owner)
        tile[...] = tile_send[...]

    arrived(h2, H2)
    for i in range(7):
        moments = moments + h2[i].astype(F32)

    @pl.when(me != row_block)
    def _():
        to_owner[0].wait_recv()

    piece = own[x, 2 * y + pair]
    share = tile[...]
    for i in range(32):
        piece = piece + share[:, i : i + 1] * moments[i : i + 1, :]
    arrived(brecv.at[pl.ds(1, 31)], RB)
    for dx, dy, dz in BLOCK:
        piece = piece + brecv[(dx * 4 + dy) * 2 + dz].astype(F32)
    piece = piece * inverse_area

    layer = lax.div(z, 2)
    strip[layer] = piece.astype(BF16)
    started([
        copy(
            strip.at[layer], strip.at[layer], SZ, SZ,
            {"cell": (lax.rem(layer + d, 8) * 2 + pair) * 4 + y},
        )
        for d in (4, 3, 5, 2, 6, 1, 7)
    ])
    started([
        copy(coarse_send.at[lax.rem(me + d, 8)], coarse_mine.at[me], CM, CM, mem_peer(d))
        for d in MEM_STEPS
    ])
    coarse_mine[pl.ds(me, 1)] = coarse_send[pl.ds(me, 1)]
    sent(psend.at[pl.ds(0, 7)], P1)
    sent(nrecv, PN)
    sent(yrecv, PY)
    sent(gsend.at[pl.ds(0, 7)], P3)
    sent(zrecv, PZ)
    sent(h1.at[pl.ds(0, 7)], H1)
    sent(h2, H2)
    sent(brecv.at[pl.ds(1, 31)], RB)
    for c in cc:
        c.wait_send()

    @pl.when(me == row_block)
    def _():
        sent(coarse_send.at[pl.ds(0, 7)], CO)

    arrived(coarse_mine.at[pl.ds(0, 7)], CM)
    sent(coarse_send.at[pl.ds(0, 7)], CM)
    columns = [jnp.broadcast_to(coarse_mine[...].reshape(128, 128)[:, k : k + 1], (128, 128)) for k in range(4)]

    def gradient(j, carry):
        lanes = pl.ds(pl.multiple_of(j * 128, 128), 128)
        key = lax.shift_right_logical(rid[:, lanes], 8)
        slope = jnp.zeros((128, 128), F32)
        for k in range(4):
            slope = jnp.where(key == k, columns[k], slope)
        part = grecv[:, :, lanes].reshape(128, 128).astype(F32)
        grad[:, lanes] = ((part + area[:, lanes] * slope) * inverse_area).astype(BF16)
        return carry

    lax.fori_loop(0, 4, gradient, 0)
    gh[0] = dot(grad[...], wp[...], 0, 0).astype(BF16)
    arrived(strip.at[pl.ds(0, 7)], SZ)
    piece = strip[0].astype(F32)
    for k in range(1, 8):
        piece = piece + strip[k].astype(F32)
    chunk = core * 4 + x
    full[chunk, row_block] = piece.astype(BF16)

    spot = full.at[chunk, row_block]
    started([copy(spot, spot, GB, GB + at[0], block_peer(*at)) for i, at in enumerate(BLOCK)])
    sent(strip.at[pl.ds(0, 7)], SZ)
    for dx in (2, 1, 3, 0):
        arrived(full.at[0, pl.ds(0, 8 if dx else 7)], GB + dx)
        spot = full.at[core * 4 + lax.rem(x - dx + 4, 4)]
        started([copy(spot, spot, GC, GC, core_peer)])
    sent(brecv.at[pl.ds(1, 31)], GB)
    arrived(full.at[pl.ds(0, 4)], GC)

    square = jnp.zeros((16, 128), F32)
    for k in range(8):
        part = full[k].astype(F32)
        square = square + jnp.sum(part * part, axis=0)
    mean_square = jnp.sum(square, keepdims=True) * (1.0 / (VARS * 1024))
    scale = lax.rsqrt(mean_square + 1e-06)
    for k in range(8):
        for j in range(8):
            rows = min(VB, VARS - VB * j)
            gw[VB * j : VB * j + rows, 128 * k : 128 * k + 128] = (full[k, j].astype(F32) * scale)[0:rows]

    sent(full.at[pl.ds(0, 4)], GC)


def write_out(gh, gw, gh_out, gw_out, done):
    copies = [pltpu.make_async_copy(gh, gh_out, done.at[0]), pltpu.make_async_copy(gw, gw_out, done.at[1])]
    for c in copies:
        c.start()
    for c in copies:
        c.wait()


def local(hidden_states, targets, cell_area, region_ids, decoder_weight):
    anywhere = pl.BlockSpec(memory_space=pl.ANY)
    vmem = pl.BlockSpec(memory_space=pltpu.VMEM)
    scratch = [
        ((512, 1024), BF16), ((VARS, 512), BF16), ((1, 512), F32), ((1, 512), I32), ((VARS, 1024), BF16),
        ((128, 1024), BF16), ((128, 512), F32), ((128, 512), BF16),
        ((8, 16, 512), BF16), ((8, 16, 512), BF16), ((8, 16, 512), BF16), ((8, 16, 512), BF16),
        ((512, 512), BF16), ((512, 512), BF16), ((512, 128), BF16), ((512, 128), BF16), ((128, 512), BF16),
        ((128, 512), F32), ((128, 512), F32), ((128, 512), F32),
        ((8, 128), F32), ((3, 8, 128), F32), ((4, 8, 128), F32), ((4, 128), F32), ((15, 4, 128), F32),
        ((4, 8, 16, 128), BF16), ((4, 8, 16, 128), BF16), ((4, 8, 16, 128), F32), ((4, 8, 16, 128), BF16),
        ((32, 16, 128), BF16), ((8, 16, 128), BF16), ((8, 8, 16, 128), BF16),
        ((8, 4, 128), F32), ((8, 4, 128), F32), ((32, 128), BF16), ((7, 32, 128), BF16),
        ((8, 16, 128), F32), ((8, 16, 128), F32), ((16, 128), F32), ((16, 128), F32), ((128, 512), BF16),
    ]
    arguments = (
        hidden_states, targets, cell_area.reshape(1, -1), region_ids.reshape(1, -1), decoder_weight.T
    )
    results = (
        jax.ShapeDtypeStruct(hidden_states.shape, BF16),
        jax.ShapeDtypeStruct((VARS, 1024), F32),
    )
    grad_hidden, grad_weight = pl.pallas_call(
        kernel,
        out_shape=results,
        in_specs=[anywhere] * 5,
        out_specs=(vmem, vmem),
        scratch_shapes=[pltpu.VMEM(s, t) for s, t in scratch]
        + [pltpu.SemaphoreType.DMA((n,)) for n in (6, COUNT, COUNT)]
        + [pltpu.SemaphoreType.REGULAR((3,))],
        compiler_params=pltpu.CompilerParams(
            collective_id=0, has_side_effects=True, vmem_limit_bytes=VMEM_LIMIT
        ),
    )(*[pltpu.with_memory_space_constraint(a, pltpu.HBM) for a in arguments])
    grad_hidden, grad_weight = pl.pallas_call(
        write_out,
        out_shape=results,
        in_specs=[vmem] * 2,
        out_specs=(anywhere, anywhere),
        scratch_shapes=[pltpu.SemaphoreType.DMA((2,))],
    )(*[pltpu.with_memory_space_constraint(a, pltpu.VMEM) for a in (grad_hidden, grad_weight)])
    return grad_hidden, grad_weight.T


def solution(mesh):
    in_specs = (P("mem", "cell", None), P(None, "cell"), P("cell"), P("cell"), P())
    out_specs = (P("mem", "cell", None), P())
    return jax.shard_map(local, mesh=mesh, in_specs=in_specs, out_specs=out_specs, check_vma=False)
```
